128 devices in a mesh: depth: 32 (over z, x, core), tile: 4 (over y).
Axes of the slice: x: 4, y: 4, z: 4, core: 2. Of those that a mesh axis runs over, the one named last changes fastest.
Arguments:
- field: float32 [64, 512, 2048], P('depth', None, 'tile'), may hold values from -6 to 6
- bin_ids: int32 [64, 512, 2048], P('depth', None, 'tile'), may hold values from 0 to 255
- table_color: bfloat16 [3, 256], replicated, may hold values from 0.02 to 1
- table_opacity: bfloat16 [256], replicated, may hold values from 0.015 to 0.15
Outputs:
- front_image: float32 [4, 512, 2048], P(None, 'depth', 'tile')
- back_image: float32 [4, 512, 2048], P(None, 'depth', 'tile')
The draws below stay inside these ranges and needn't reach their ends.
All inputs are finite; a program needn't handle non-finite values.
Results may differ from the reference program's by a relative error of at most 0.0003.
Values sent between devices are 32-bit elements; how exact they have to be, the bound alone decides.
A program may use at most 128 MiB of HBM per device.

```python
import math
import jax
import jax.numpy as jnp
from jax import lax

ROWS = 512
BINS = 256
DEPTH = 64
COLS = 2048


def draw_bin_ids(key, part):
    key = jax.random.fold_in(key, 11)
    first_key, second_key, third_key = jax.random.split(key, 3)
    shape = (DEPTH, ROWS, COLS)
    half_bins = BINS // 2
    within = jax.random.randint(first_key, shape, 0, half_bins)
    depth_odd = lax.broadcasted_iota(jnp.int32, shape, 0) % 2
    layered = within + half_bins * depth_odd
    anywhere = jax.random.randint(second_key, shape, 0, BINS)
    stray = jax.random.randint(third_key, shape, 0, 8) == 0
    return jnp.where(stray, anywhere, layered).astype(jnp.int32)


def draw_table_color(key, part):
    key = jax.random.fold_in(key, 12)
    channel = lax.broadcasted_iota(jnp.int32, (3, BINS), 0)
    bin_index = lax.broadcasted_iota(jnp.int32, (3, BINS), 1)
    upper = bin_index >= BINS // 2
    heavy = jnp.where(upper, 2, 0)
    light = jnp.where(upper, 0, 2)
    heavy_lo, heavy_hi, light_lo, light_hi = (0.7, 1.0, 0.05, 0.3)
    lower_end = jnp.where(channel == heavy, heavy_lo, jnp.where(channel == light, light_lo, 0.3))
    upper_end = jnp.where(channel == heavy, heavy_hi, jnp.where(channel == light, light_hi, 0.7))
    unit = jax.random.uniform(key, (3, BINS), jnp.float32)
    return (lower_end + (upper_end - lower_end) * unit).astype(jnp.bfloat16)


def draw_table_opacity(key, part):
    key = jax.random.fold_in(key, 13)
    logs = jax.random.uniform(key, (BINS,), jnp.float32, math.log(0.015), math.log(0.15))
    values = jnp.exp(logs)
    return values.astype(jnp.bfloat16)


def block_levels(own_key, dims, cuts, smallest, high):
    def one(position, parts):
        draws = jax.random.uniform(jax.random.fold_in(jax.random.fold_in(own_key, 6), position), (parts,), jnp.float32, smallest / len(cuts), high / len(cuts))
        return jnp.repeat(jnp.exp(draws), dims[position] // parts).reshape((-1,) + (1,) * (len(dims) - position - 1))

    factor_of = one(*cuts[0])
    for cut in cuts[1:]:
        factor_of = factor_of * one(*cut)
    return factor_of


def bell_draw(own_key, extent, deviation, most, pieces=(), kind=jnp.bfloat16):
    result = deviation * jax.random.normal(own_key, extent, jnp.float32)
    if pieces:
        result = result * block_levels(own_key, extent, pieces, -0.22, 0.18)
    return jnp.clip(result, -most, most).astype(kind)


def setup_inputs(seed: int = 0) -> dict:
    arg_keys = jax.random.split(jax.random.key(seed), 5)
    return {
        "field": bell_draw(arg_keys[0], (DEPTH, ROWS, COLS), 1.0, 6.0, ((0, 32), (2, 4)), jnp.float32),
        "bin_ids": draw_bin_ids(jax.random.fold_in(arg_keys[4], 71), 0),
        "table_color": draw_table_color(jax.random.fold_in(arg_keys[4], 71), 0),
        "table_opacity": draw_table_opacity(jax.random.fold_in(arg_keys[4], 71), 0),
    }


def four_point(lower_two, lower_one, upper_one, upper_two):
    return (lower_two - 8.0 * lower_one + 8.0 * upper_one - upper_two) / 12.0

def shade(padded, colors, opacity):
    slabs = padded.shape[0] - 4
    height = padded.shape[1] - 4
    columns = padded.shape[2] - 4
    grad_depth = four_point(padded[0:slabs, 2:height + 2, 2:columns + 2], padded[1:slabs + 1, 2:height + 2, 2:columns + 2], padded[3:slabs + 3, 2:height + 2, 2:columns + 2], padded[4:slabs + 4, 2:height + 2, 2:columns + 2])
    grad_rows = four_point(padded[2:slabs + 2, 0:height, 2:columns + 2], padded[2:slabs + 2, 1:height + 1, 2:columns + 2], padded[2:slabs + 2, 3:height + 3, 2:columns + 2], padded[2:slabs + 2, 4:height + 4, 2:columns + 2])
    grad_cols = four_point(padded[2:slabs + 2, 2:height + 2, 0:columns], padded[2:slabs + 2, 2:height + 2, 1:columns + 1], padded[2:slabs + 2, 2:height + 2, 3:columns + 3], padded[2:slabs + 2, 2:height + 2, 4:columns + 4])
    grad_sq = grad_depth * grad_depth + grad_rows * grad_rows + grad_cols * grad_cols
    lambert = 0.3 + 0.7 * jnp.abs(0.48 * grad_depth + 0.6 * grad_rows + 0.64 * grad_cols) / jnp.sqrt(grad_sq + 1.0)
    sample_alpha = opacity * grad_sq / (grad_sq + 1.0)
    sample_color = colors * (sample_alpha * lambert)[None]
    return (sample_color, sample_alpha)

def march(sample_color, sample_alpha, backward):
    height = sample_alpha.shape[1]
    columns = sample_alpha.shape[2]

    def advance(state, sample):
        accumulated, transmit = state
        color_slice, alpha_slice = sample
        return ((accumulated + transmit[None] * color_slice, transmit * (1.0 - alpha_slice)), None)
    start = (jnp.zeros((3, height, columns), jnp.float32), jnp.ones((height, columns), jnp.float32))
    final, _ = lax.scan(advance, start, (jnp.moveaxis(sample_color, 1, 0), sample_alpha), reverse=backward)
    return jnp.concatenate([final[0], final[1][None]], axis=0)

def reference(field, bin_ids, table_color, table_opacity):
    padded = jnp.pad(field, 2)
    colors = jnp.take(table_color.astype(jnp.float32), bin_ids, axis=1)
    opacity = jnp.take(table_opacity.astype(jnp.float32), bin_ids, axis=0)
    sample_color, sample_alpha = shade(padded, colors, opacity)
    return (march(sample_color, sample_alpha, False), march(sample_color, sample_alpha, True))
```

```python
import jax
import jax.numpy as jnp
from jax import lax
from jax.experimental import pallas as pl
from jax.experimental.pallas import tpu as pltpu
from jax.sharding import PartitionSpec as P

MESH = pl.DeviceIdType.MESH
F32 = jnp.float32
NZ, NX, NC = 4, 4, 2
NB = NZ // NC
NS = 2 * NX * NC
BR = 32
NT = 4
TOP = 8


def kernel(
    field, bins, tcol, topa, front, back,
    fb, bb, hb, hs, fv, stage, img,
    lsem, fsem, bsem, hsem, zsem, ysem, isem, sf, sb, sh, sz, sy, si,
):
    d = lax.axis_index("depth")
    y = lax.axis_index("tile")
    z = d // (NX * NC)
    xc = d % (NX * NC)
    x = xc // NC
    c = xc % NC
    ny = lax.axis_size("tile")

    def dev(z_, x_, c_):
        return (z_ * (NX * NC) + x_ * NC + c_, y)

    load = pltpu.make_async_copy(field, fv, lsem.at[0])
    load.start()
    bar = pltpu.get_barrier_semaphore()
    for p in range(1, NX * NC):
        q = (xc + p) % (NX * NC)
        pl.semaphore_signal(bar, inc=1, device_id=(z * (NX * NC) + q, y), device_id_type=MESH)
    for p in range(1, NZ):
        for c_ in range(NC):
            pl.semaphore_signal(bar, inc=1, device_id=dev((z + p) % NZ, x, c_), device_id_type=MESH)
    for p in (1, ny - 1):
        pl.semaphore_signal(bar, inc=1, device_id=(d, (y + p) % ny), device_id_type=MESH)

    @pl.when(y == 0)
    def _():
        fb[:, 0, 2:2 + NS, TOP:TOP + BR, :] = jnp.zeros((NB, NS, BR, 128), F32)

    @pl.when(y == ny - 1)
    def _():
        fb[:, NT + 1, 2:2 + NS, TOP:TOP + BR, :] = jnp.zeros((NB, NS, BR, 128), F32)

    @pl.when(z == 0)
    def _():
        fb[:, 1:NT + 1, 0:2, TOP:TOP + BR, :] = jnp.zeros((NB, NT, 2, BR, 128), F32)

    @pl.when(z == NZ - 1)
    def _():
        fb[:, 1:NT + 1, NS + 2:NS + 4, TOP:TOP + BR, :] = jnp.zeros((NB, NT, 2, BR, 128), F32)

    pl.semaphore_wait(bar, NX * NC - 1 + (NZ - 1) * NC + 2)

    def piece(step, x_, c_):
        b, t = step // NT, step % NT
        j = (3 * t) % NT
        row = ((c_ * NB + b) * NX + x_) * BR
        rows = pl.ds(pl.multiple_of(row, BR), BR)
        cols = pl.ds(pl.multiple_of(j * 128, 128), 128)
        return b, j, rows, cols

    def x_copies(step, p):
        q = (xc + p) % (NX * NC)
        x_, c_ = q // NC, q % NC
        b, j, rows, cols = piece(step, x_, c_)
        to = (z * (NX * NC) + q, y)
        f = pltpu.make_async_remote_copy(
            src_ref=field.at[:, rows, cols],
            dst_ref=fb.at[b, j + 1, pl.ds(2 + 2 * xc, 2), pl.ds(TOP, BR), :],
            send_sem=sf.at[step, p], recv_sem=fsem.at[step], device_id=to, device_id_type=MESH)
        g = pltpu.make_async_remote_copy(
            src_ref=bins.at[:, rows, cols],
            dst_ref=bb.at[b, j, pl.ds(2 * xc, 2), :, :],
            send_sem=sb.at[step, p], recv_sem=bsem.at[step], device_id=to, device_id_type=MESH)
        return f, g

    def own_copies(step):
        b, j, rows, cols = piece(step, x, c)
        f = pltpu.make_async_copy(
            field.at[:, rows, cols],
            fb.at[b, j + 1, pl.ds(2 + 2 * xc, 2), pl.ds(TOP, BR), :], fsem.at[step])
        g = pltpu.make_async_copy(
            bins.at[:, rows, cols], bb.at[b, j, pl.ds(2 * xc, 2), :, :], bsem.at[step])
        return f, g

    def h_copy(b, p):
        q = (xc + p) % (NX * NC)
        x_, c_ = q // NC, q % NC
        k = (c_ * NB + b) * NX + x_
        return pltpu.make_async_remote_copy(
            src_ref=hs.at[k], dst_ref=hb.at[b, xc],
            send_sem=sh.at[b, p], recv_sem=hsem.at[b],
            device_id=(z * (NX * NC) + q, y), device_id_type=MESH)

    def h_own(b):
        k = (c * NB + b) * NX + x
        return pltpu.make_async_copy(hs.at[k], hb.at[b, xc], hsem.at[b])

    def send_step(step, carry=0):
        for cp in own_copies(step):
            cp.start()

        def one(p, k):
            for cp in x_copies(step, p):
                cp.start()
            return k

        lax.fori_loop(1, NX * NC, one, 0)
        return carry

    send_step(0)
    send_step(1)

    load.wait()
    nk = NX * NZ
    for k in range(nk):
        for s in range(2):
            for j in range(NT):
                lanes = slice(128 * j, 128 * j + 128)
                if k == 0:
                    hs[k, j, 4 * s:4 * s + 2, :] = jnp.zeros((2, 128), F32)
                else:
                    hs[k, j, 4 * s:4 * s + 2, :] = fv[s, BR * k - 2:BR * k, lanes]
                if k == nk - 1:
                    hs[k, j, 4 * s + 2:4 * s + 4, :] = jnp.zeros((2, 128), F32)
                else:
                    hs[k, j, 4 * s + 2:4 * s + 4, :] = fv[s, BR * k + BR:BR * k + BR + 2, lanes]

    def send_h(b):
        h_own(b).start()

        def one(p, k):
            h_copy(b, p).start()
            return k

        lax.fori_loop(1, NX * NC, one, 0)

    send_h(0)
    lax.fori_loop(2, NB * NT - 1, send_step, 0)
    send_h(1)
    send_step(NB * NT - 1)

    tc = tcol[...].astype(F32)
    to_ = topa[...].astype(F32) * (1.0 / 144.0)
    tabs = []
    for k in range(3):
        tabs.append([jnp.broadcast_to(tc[k:k + 1, 128 * h:128 * h + 128], (8, 128)) for h in range(2)])
    tabs.append([jnp.broadcast_to(to_[:, 128 * h:128 * h + 128], (8, 128)) for h in range(2)])

    def z_copy(step, up):
        b, t = step // NT, step % NT
        j = (3 * t) % NT
        src = fb.at[b, j + 1, pl.ds(NS if up else 2, 2), pl.ds(TOP, BR), :]
        dst = fb.at[b, j + 1, pl.ds(0 if up else NS + 2, 2), pl.ds(TOP, BR), :]
        return pltpu.make_async_remote_copy(
            src_ref=src, dst_ref=dst, send_sem=sz.at[step, int(up)], recv_sem=zsem.at[step, int(up)],
            device_id=(d + (NX * NC if up else -NX * NC), y), device_id_type=MESH)

    def y_copy(b, right):
        src = fb.at[b, NT if right else 1, pl.ds(2, NS), pl.ds(TOP, BR), :]
        dst = fb.at[b, 0 if right else NT + 1, pl.ds(2, NS), pl.ds(TOP, BR), :]
        return pltpu.make_async_remote_copy(
            src_ref=src, dst_ref=dst, send_sem=sy.at[b, int(right)], recv_sem=ysem.at[b, int(right)],
            device_id=(d, y + (1 if right else -1)), device_id_type=MESH)

    def arrive(step):
        b, t = step // NT, step % NT
        j = (3 * t) % NT
        fr = fb.at[b, j + 1, pl.ds(2, NS), pl.ds(TOP, BR), :]
        pltpu.make_async_copy(fr, fr, fsem.at[step]).wait()
        br = bb.at[b, j]
        pltpu.make_async_copy(br, br, bsem.at[step]).wait()

        @pl.when(z < NZ - 1)
        def _():
            z_copy(step, True).start()

        @pl.when(z > 0)
        def _():
            z_copy(step, False).start()

        if t == 0:
            @pl.when(y > 0)
            def _():
                y_copy(b, False).start()
        if t == 1:
            @pl.when(y < ny - 1)
            def _():
                y_copy(b, True).start()

    def z_wait(step):
        @pl.when(z > 0)
        def _():
            z_copy(step, True).wait_recv()

        @pl.when(z < NZ - 1)
        def _():
            z_copy(step, False).wait_recv()

    def y_wait(b):
        @pl.when(y > 0)
        def _():
            y_copy(b, True).wait_recv()

        @pl.when(y < ny - 1)
        def _():
            y_copy(b, False).wait_recv()

    def rows_in(b):
        hr = hb.at[b]
        pltpu.make_async_copy(hr, hr, hsem.at[b]).wait()

        def one(i, k):
            for j in range(NT):
                for s in range(2):
                    fb[b, j + 1, 2 + 2 * i + s, TOP - 2:TOP, :] = hb[b, i, j, 4 * s:4 * s + 2, :]
                    fb[b, j + 1, 2 + 2 * i + s, TOP + BR:TOP + BR + 2, :] = hb[b, i, j, 4 * s + 2:4 * s + 4, :]
            return k

        lax.fori_loop(0, NX * NC, one, 0)

    lane = lax.broadcasted_iota(jnp.int32, (8, 128), 1)
    kd, kr, kc = 0.7 * 0.48 / 12.0, 0.7 * 0.6 / 12.0, 0.7 * 0.64 / 12.0

    def shade(b, j, g):
        r = pl.multiple_of(TOP + 8 * g, 8)
        win = [fb[b, j + 1, s, pl.ds(r, 8), :] for s in range(4)]
        fr = [jnp.zeros((8, 128), F32) for _ in range(3)]
        bk = [jnp.zeros((8, 128), F32) for _ in range(3)]
        tr = jnp.ones((8, 128), F32)
        for s in range(NS):
            win.append(fb[b, j + 1, s + 4, pl.ds(r, 8), :])
            v = win[s + 2]
            gd = 8.0 * (win[s + 3] - win[s + 1]) + (win[s] - win[s + 4])
            m2, m1, p1, p2 = [fb[b, j + 1, s + 2, pl.ds(r + o, 8), :] for o in (-2, -1, 1, 2)]
            gr = 8.0 * (p1 - m1) + (m2 - p2)
            lt = fb[b, j, s + 2, pl.ds(r, 8), :]
            rt = fb[b, j + 2, s + 2, pl.ds(r, 8), :]
            l1 = pltpu.roll(jnp.where(lane == 127, lt, v), 1, 1)
            l2 = pltpu.roll(jnp.where(lane >= 126, lt, v), 2, 1)
            r1 = pltpu.roll(jnp.where(lane == 0, rt, v), 127, 1)
            r2 = pltpu.roll(jnp.where(lane < 2, rt, v), 126, 1)
            gc = 8.0 * (r1 - l1) + (l2 - r2)
            ids = bb[b, j, s, pl.ds(pl.multiple_of(8 * g, 8), 8), :]
            low = ids & 127
            upper = ids >= 128
            look = [
                jnp.where(upper,
                          jnp.take_along_axis(hi, low, axis=1, mode="promise_in_bounds"),
                          jnp.take_along_axis(lo, low, axis=1, mode="promise_in_bounds"))
                for lo, hi in tabs
            ]
            q = gd * gd + gr * gr + gc * gc
            inv = lax.rsqrt(q * (1.0 / 144.0) + 1.0)
            alpha = look[3] * (q * (inv * inv))
            lam = 0.3 + jnp.abs(kd * gd + kr * gr + kc * gc) * inv
            w = alpha * lam
            keep = 1.0 - alpha
            for k in range(3):
                col = look[k] * w
                fr[k] = fr[k] + tr * col
                bk[k] = bk[k] * keep + col
            tr = tr * keep
        rows = pl.ds(pl.multiple_of(8 * g, 8), 8)
        for k in range(3):
            stage[b, j, k, rows, :] = fr[k]
            stage[b, j, 3 + k, rows, :] = bk[k]
        stage[b, j, 6, rows, :] = tr

    def i_copy(b, j, c_):
        return pltpu.make_async_remote_copy(
            src_ref=stage.at[b, j, :, pl.ds(16 * c_, 16), :], dst_ref=img.at[z, j],
            send_sem=si.at[b, j, c_], recv_sem=isem.at[z, j],
            device_id=dev(c * NB + b, x, c_), device_id_type=MESH)

    def i_own(b, j, c_):
        return pltpu.make_async_copy(
            stage.at[b, j, :, pl.ds(16 * c_, 16), :], img.at[z, j], isem.at[z, j])

    def item(b, j):
        def group(g, k):
            shade(b, j, g)
            return k

        lax.fori_loop(0, BR // 8, group, 0)
        for c_ in range(NC):
            mine = jnp.logical_and(z == c * NB + b, c == c_)

            @pl.when(mine)
            def _():
                i_own(b, j, c_).start()

            @pl.when(jnp.logical_not(mine))
            def _():
                i_copy(b, j, c_).start()

    for step in range(NT + 1):
        arrive(step)
    rows_in(0)
    y_wait(0)
    for step in range(NT):
        z_wait(step)

    def first(m, k):
        item(0, (3 * m) % NT)
        return k

    lax.fori_loop(0, NT, first, 0)
    arrive(NT + 1)
    arrive(NT + 2)
    rows_in(1)
    y_wait(1)
    z_wait(NT)
    z_wait(NT + 1)

    def second(m, k):
        @pl.when(m == 1)
        def _():
            arrive(NT + 3)
            z_wait(NT + 2)

        @pl.when(m == 3)
        def _():
            z_wait(NT + 3)

        item(1, 3 - m - m // 2 + 2 * (m // 3))
        return k

    lax.fori_loop(0, NT, second, 0)

    for j in range(NT):
        parts = []
        for s in range(NZ):
            ir = img.at[s, j]
            pltpu.make_async_copy(ir, ir, isem.at[s, j]).wait()
        lanes = slice(128 * j, 128 * j + 128)
        ts = [img[s, j, 6] for s in range(NZ)]
        for k in range(3):
            acc = img[NZ - 1, j, k]
            for s in range(NZ - 2, -1, -1):
                acc = img[s, j, k] + ts[s] * acc
            front[k, :, lanes] = acc
            acc = img[0, j, 3 + k]
            for s in range(1, NZ):
                acc = img[s, j, 3 + k] + ts[s] * acc
            back[k, :, lanes] = acc
        t = (ts[0] * ts[1]) * (ts[2] * ts[3])
        front[3, :, lanes] = t
        back[3, :, lanes] = t

    def drain(step, k):
        def one(p, k2):
            for cp in x_copies(step, p):
                cp.wait_send()
            return k2

        lax.fori_loop(1, NX * NC, one, 0)

        @pl.when(z < NZ - 1)
        def _():
            z_copy(step, True).wait_send()

        @pl.when(z > 0)
        def _():
            z_copy(step, False).wait_send()
        return k

    lax.fori_loop(0, NB * NT, drain, 0)
    for b in range(NB):
        def one(p, k2):
            h_copy(b, p).wait_send()
            return k2

        lax.fori_loop(1, NX * NC, one, 0)

        @pl.when(y > 0)
        def _():
            y_copy(b, False).wait_send()

        @pl.when(y < ny - 1)
        def _():
            y_copy(b, True).wait_send()

        for j in range(NT):
            for c_ in range(NC):
                @pl.when(jnp.logical_not(jnp.logical_and(z == c * NB + b, c == c_)))
                def _():
                    i_copy(b, j, c_).wait_send()


def local(field, bin_ids, table_color, table_opacity):
    cols = field.shape[2]
    out = jax.ShapeDtypeStruct((4, 16, cols), F32)
    vm = pl.BlockSpec(memory_space=pltpu.VMEM)
    hbm = pl.BlockSpec(memory_space=pl.ANY)
    dma = pltpu.SemaphoreType.DMA
    steps = NB * NT
    return pl.pallas_call(
        kernel,
        out_shape=(out, out),
        in_specs=[hbm, hbm, vm, vm],
        out_specs=(vm, vm),
        scratch_shapes=[
            pltpu.VMEM((NB, NT + 2, NS + 4, BR + 16, 128), F32),
            pltpu.VMEM((NB, NT, NS, BR, 128), jnp.int32),
            pltpu.VMEM((NB, NX * NC, NT, 8, 128), F32),
            pltpu.VMEM((NX * NZ, NT, 8, 128), F32),
            pltpu.VMEM(field.shape, F32),
            pltpu.VMEM((NB, NT, 7, BR, 128), F32),
            pltpu.VMEM((NZ, NT, 7, 16, 128), F32),
            dma((1,)), dma((steps,)), dma((steps,)), dma((NB,)), dma((steps, 2)), dma((NB, 2)), dma((NZ, NT)),
            dma((steps, NX * NC)), dma((steps, NX * NC)), dma((NB, NX * NC)), dma((steps, 2)), dma((NB, 2)),
            dma((NB, NT, NC)),
        ],
        compiler_params=pltpu.CompilerParams(
            collective_id=0, has_side_effects=True, vmem_limit_bytes=40 * 2**20),
    )(field, bin_ids, table_color, table_opacity.reshape(1, -1))


def solution(mesh):
    return jax.shard_map(
        local,
        mesh=mesh,
        in_specs=(P("depth", None, "tile"), P("depth", None, "tile"), P(), P()),
        out_specs=(P(None, "depth", "tile"), P(None, "depth", "tile")),
        check_vma=False,
    )
```

```python
import jax
import jax.numpy as jnp
from jax import lax
from jax.experimental import pallas as pl
from jax.experimental.pallas import tpu as pltpu
from jax.sharding import PartitionSpec as P

MESH = pl.DeviceIdType.MESH
F32 = jnp.float32
NZ, NX, NC = 4, 4, 2
NR = NX * NC
NS = 2 * NR
BR = 16
NT = 4
TOP = 8
HALF = NZ * NT


def kernel(
    field, bins, tcol_h, topa_h, front, back,
    tcol, topa, fb, bb, hb, hs, fv, ga, gl, stage, img,
    lsem, fsem, bsem, hsem, zsem, ysem, csem, isem, sx, sh, sz, sy, sc, si,
):
    d = lax.axis_index("depth")
    y = lax.axis_index("tile")
    ny = lax.axis_size("tile")
    z = d // NR
    xc = d % NR
    x = xc // NC
    c = xc % NC

    load = pltpu.make_async_copy(field, fv, lsem.at[0])
    load.start()
    tload = [pltpu.make_async_copy(tcol_h, tcol, lsem.at[1]), pltpu.make_async_copy(topa_h, topa, lsem.at[2])]
    for cp in tload:
        cp.start()
    bar = pltpu.get_barrier_semaphore()
    for p in range(1, NR):
        pl.semaphore_signal(bar, inc=1, device_id=(z * NR + (xc + p) % NR, y), device_id_type=MESH)
    for p in range(1, NZ):
        pl.semaphore_signal(bar, inc=1, device_id=((z + p) % NZ * NR + xc, y), device_id_type=MESH)
    for p in (1, ny - 1):
        pl.semaphore_signal(bar, inc=1, device_id=(d, (y + p) % ny), device_id_type=MESH)

    @pl.when(y == 0)
    def _():
        fb[:, 0, 2:2 + NS, TOP:TOP + BR, :] = jnp.zeros((NZ, NS, BR, 128), F32)

    @pl.when(y == ny - 1)
    def _():
        fb[:, NT + 1, 2:2 + NS, TOP:TOP + BR, :] = jnp.zeros((NZ, NS, BR, 128), F32)

    @pl.when(z == 0)
    def _():
        fb[:, 1:NT + 1, 0:2, TOP:TOP + BR, :] = jnp.zeros((NZ, NT, 2, BR, 128), F32)

    @pl.when(z == NZ - 1)
    def _():
        fb[:, 1:NT + 1, NS + 2:NS + 4, TOP:TOP + BR, :] = jnp.zeros((NZ, NT, 2, BR, 128), F32)

    pl.semaphore_wait(bar, NR - 1 + NZ - 1 + 2)

    def rows_of(zb, q):
        return pl.ds(pl.multiple_of((zb * NX + q // NC) * BR * NC + q % NC * BR, BR), BR)

    def copy_x(src, dst, send, recv, q):
        return pltpu.make_async_remote_copy(
            src_ref=src, dst_ref=dst, send_sem=send, recv_sem=recv,
            device_id=(z * NR + q, y), device_id_type=MESH)

    def bin_tile(m):
        t = m // NT
        mixed = (t % 3 + 1) // 2
        off = mixed * (1 + 2 * (m % 2)) + (1 - mixed) * 2 * (1 - t // 3)
        return (z + off) % NZ, mixed * ((m - NT) // 2) + (1 - mixed) * (m % NT)

    def tick_refs(n, q):
        f_zb, f_j = n // NT, n % NT
        b_zb, b_j = bin_tile(n - HALF)
        f_cols = pl.ds(pl.multiple_of(128 * f_j, 128), 128)
        b_cols = pl.ds(pl.multiple_of(128 * b_j, 128), 128)
        return (
            (field.at[:, rows_of(f_zb, q), f_cols], fb.at[f_zb, f_j + 1, pl.ds(2 + 2 * xc, 2), pl.ds(TOP, BR), :]),
            (bins.at[:, rows_of(b_zb, q), b_cols], bb.at[b_zb, pl.ds(2 * xc, 2), :, b_cols]),
        )

    def send_tick(n, k=0):
        for kind in range(2):
            @pl.when(n // HALF == kind)
            def _():
                recv = bsem.at[n - HALF] if kind else fsem.at[n // NT]
                src, dst = tick_refs(n, xc)[kind]
                pltpu.make_async_copy(src, dst, recv).start()

                def one(p, k2):
                    q = (xc + p) % NR
                    src, dst = tick_refs(n, q)[kind]
                    copy_x(src, dst, sx.at[n], recv, q).start()
                    return k2

                lax.fori_loop(1, NR, one, 0)
        return k

    def tick_left(n):
        some = bb.at[0, pl.ds(0, NS - 2), :, pl.ds(0, 128)]
        pltpu.make_async_copy(some, some, sx.at[n]).wait()

    def send_h():
        pltpu.make_async_copy(hs.at[xc], hb.at[xc], hsem.at[0]).start()

        def one(p, k):
            q = (xc + p) % NR
            copy_x(hs.at[q], hb.at[xc], sh.at[0], hsem.at[0], q).start()
            return k

        lax.fori_loop(1, NR, one, 0)

    lax.fori_loop(0, NT, send_tick, 0)

    load.wait()
    total = NZ * NX * NC * BR
    for q in range(NR):
        for zb in range(NZ):
            r0 = (zb * NX + q // NC) * BR * NC + (BR * NC if q % NC else -2)
            for s in range(2):
                o = zb % 2 * 4 + s * 2
                for j in range(NT):
                    if 0 <= r0 < total:
                        hs[q, zb // 2, j, o:o + 2, :] = fv[s, r0:r0 + 2, 128 * j:128 * j + 128]
                    else:
                        hs[q, zb // 2, j, o:o + 2, :] = jnp.zeros((2, 128), F32)

    send_h()
    lax.fori_loop(NT, 2 * HALF, send_tick, 0)

    for cp in tload:
        cp.wait()
    tc = tcol[...].astype(F32)
    to_ = topa[...].astype(F32).reshape(1, -1) * (1.0 / 144.0)
    tabs = []
    for k in range(3):
        tabs.append([jnp.broadcast_to(tc[k:k + 1, 128 * h:128 * h + 128], (8, 128)) for h in range(2)])
    tabs.append([jnp.broadcast_to(to_[:, 128 * h:128 * h + 128], (8, 128)) for h in range(2)])

    def z_copy(zb, up):
        src = fb.at[zb, pl.ds(1, NT), pl.ds(NS if up else 2, 2), pl.ds(TOP, BR), :]
        dst = fb.at[zb, pl.ds(1, NT), pl.ds(0 if up else NS + 2, 2), pl.ds(TOP, BR), :]
        return pltpu.make_async_remote_copy(
            src_ref=src, dst_ref=dst, send_sem=sz.at[zb, int(up)], recv_sem=zsem.at[zb, int(up)],
            device_id=(d + (NR if up else -NR), y), device_id_type=MESH)

    def y_copy(zb, right):
        src = fb.at[zb, NT if right else 1, pl.ds(2, NS), pl.ds(TOP, BR), :]
        dst = fb.at[zb, 0 if right else NT + 1, pl.ds(2, NS), pl.ds(TOP, BR), :]
        return pltpu.make_async_remote_copy(
            src_ref=src, dst_ref=dst, send_sem=sy.at[zb, int(right)], recv_sem=ysem.at[zb, int(right)],
            device_id=(d, y + (1 if right else -1)), device_id_type=MESH)

    def c_copy(zb):
        src = fb.at[zb, pl.ds(1, NT), pl.ds(2, NS), pl.ds(pl.multiple_of(TOP + 8 * (1 - c), 8), 8), :]
        dst = fb.at[zb, pl.ds(1, NT), pl.ds(2, NS), pl.ds(pl.multiple_of((TOP + BR) * c, 8), 8), :]
        return pltpu.make_async_remote_copy(
            src_ref=src, dst_ref=dst, send_sem=sc.at[zb], recv_sem=csem.at[zb],
            device_id=(d + 1 - 2 * c, y), device_id_type=MESH)

    def pass_on(zb):
        own = fb.at[zb, pl.ds(1, NT), pl.ds(2, NS), pl.ds(TOP, BR), :]
        pltpu.make_async_copy(own, own, fsem.at[zb]).wait()

        @pl.when(z < NZ - 1)
        def _():
            z_copy(zb, True).start()

        @pl.when(z > 0)
        def _():
            z_copy(zb, False).start()

        @pl.when(y > 0)
        def _():
            y_copy(zb, False).start()

        @pl.when(y < ny - 1)
        def _():
            y_copy(zb, True).start()

        c_copy(zb).start()

    def rows_in(i, k, at):
        for zb in range(NZ):
            for s in range(2):
                a = zb % 2 * 4 + s * 2
                for j in range(NT):
                    fb[zb, j + 1, 2 + 2 * i + s, at:at + 2, :] = hb[i, zb // 2, j, a:a + 2, :]
        return k

    def all_rows_in():
        pltpu.make_async_copy(hb, hb, hsem.at[0]).wait()

        @pl.when(c == 0)
        def _():
            lax.fori_loop(0, NR, lambda i, k: rows_in(i, k, TOP - 2), 0)

        @pl.when(c == 1)
        def _():
            lax.fori_loop(0, NR, lambda i, k: rows_in(i, k, TOP + BR), 0)

    def halos(zb):
        @pl.when(z > 0)
        def _():
            z_copy(zb, True).wait_recv()

        @pl.when(z < NZ - 1)
        def _():
            z_copy(zb, False).wait_recv()

        @pl.when(y > 0)
        def _():
            y_copy(zb, True).wait_recv()

        @pl.when(y < ny - 1)
        def _():
            y_copy(zb, False).wait_recv()

        c_copy(zb).wait_recv()

    lane = lax.broadcasted_iota(jnp.int32, (8, 128), 1)
    kd, kr, kc = 0.7 * 0.48 / 12.0, 0.7 * 0.6 / 12.0, 0.7 * 0.64 / 12.0

    def gradients(zb, j, g):
        r = pl.multiple_of(TOP + 8 * g, 8)
        rows = pl.ds(pl.multiple_of(8 * g, 8), 8)
        lanes = pl.ds(pl.multiple_of(128 * j, 128), 128)
        win = [fb[zb, j + 1, s, pl.ds(r, 8), :] for s in range(4)]
        for s in range(NS):
            win.append(fb[zb, j + 1, s + 4, pl.ds(r, 8), :])
            v = win[s + 2]
            gd = 8.0 * (win[s + 3] - win[s + 1]) + (win[s] - win[s + 4])
            m2, m1, p1, p2 = [fb[zb, j + 1, s + 2, pl.ds(r + o, 8), :] for o in (-2, -1, 1, 2)]
            gr = 8.0 * (p1 - m1) + (m2 - p2)
            lt = fb[zb, j, s + 2, pl.ds(r, 8), :]
            rt = fb[zb, j + 2, s + 2, pl.ds(r, 8), :]
            l1 = pltpu.roll(jnp.where(lane == 127, lt, v), 1, 1)
            l2 = pltpu.roll(jnp.where(lane >= 126, lt, v), 2, 1)
            r1 = pltpu.roll(jnp.where(lane == 0, rt, v), 127, 1)
            r2 = pltpu.roll(jnp.where(lane < 2, rt, v), 126, 1)
            gc = 8.0 * (r1 - l1) + (l2 - r2)
            q = gd * gd + gr * gr + gc * gc
            inv = lax.rsqrt(q * (1.0 / 144.0) + 1.0)
            a = q * (inv * inv)
            ga[zb, s, rows, lanes] = a
            gl[zb, s, rows, lanes] = a * (0.3 + jnp.abs(kd * gd + kr * gr + kc * gc) * inv)

    def shade(zb, j, g, m):
        rows = pl.ds(pl.multiple_of(8 * g, 8), 8)
        lanes = pl.ds(pl.multiple_of(128 * j, 128), 128)
        fr = [jnp.zeros((8, 128), F32) for _ in range(3)]
        bk = [jnp.zeros((8, 128), F32) for _ in range(3)]
        tr = jnp.ones((8, 128), F32)
        for s in range(NS):
            ids = bb[zb, s, rows, lanes]
            low = ids & 127
            upper = ids >= 128
            look = [
                jnp.where(upper,
                          jnp.take_along_axis(hi, low, axis=1, mode="promise_in_bounds"),
                          jnp.take_along_axis(lo, low, axis=1, mode="promise_in_bounds"))
                for lo, hi in tabs
            ]
            keep = 1.0 - look[3] * ga[zb, s, rows, lanes]
            w = look[3] * gl[zb, s, rows, lanes]
            for k in range(3):
                col = look[k] * w
                fr[k] = fr[k] + tr * col
                bk[k] = bk[k] * keep + col
            tr = tr * keep
        for k, part in enumerate(fr + bk + [tr]):
            stage[m, k, rows, :] = part

    def i_copy(m):
        zb, j = bin_tile(m)
        return pltpu.make_async_remote_copy(
            src_ref=stage.at[m], dst_ref=img.at[z, j], send_sem=si.at[m], recv_sem=isem.at[z, j],
            device_id=(zb * NR + xc, y), device_id_type=MESH)

    def finish(m):
        j = m % NT
        img[z, j] = stage[m]
        for p in range(1, NZ):
            other = img.at[(z + p) % NZ, j]
            pltpu.make_async_copy(other, other, isem.at[(z + p) % NZ, j]).wait()
        lanes = pl.ds(pl.multiple_of(128 * j, 128), 128)
        ts = [img[s, j, 6] for s in range(NZ)]
        t = (ts[0] * ts[1]) * (ts[2] * ts[3])
        for n in range(3):
            acc = img[NZ - 1, j, n]
            for s in range(NZ - 2, -1, -1):
                acc = img[s, j, n] + ts[s] * acc
            front[n, :, lanes] = acc
            acc = img[0, j, 3 + n]
            for s in range(1, NZ):
                acc = img[s, j, 3 + n] + ts[s] * acc
            back[n, :, lanes] = acc
        front[3, :, lanes] = t
        back[3, :, lanes] = t

    def cells_in(n, k):
        pl.when(n < NZ)(lambda: pass_on(n))
        pl.when(n == 1)(all_rows_in)

        @pl.when(n > 0)
        def _():
            halos(n - 1)

            def part(h, k2):
                gradients(n - 1, h // 2, h % 2)
                return k2

            lax.fori_loop(0, 2 * NT, part, 0)
        return k

    lax.fori_loop(0, NZ + 1, cells_in, 0)

    def bins_in(m, k):
        zb, j = bin_tile(m)
        got = bb.at[zb, :, :, pl.ds(pl.multiple_of(128 * j, 128), 128)]
        pltpu.make_async_copy(got, got, bsem.at[m]).wait()

        def part(h, k2):
            shade(zb, j, h, m)
            return k2

        lax.fori_loop(0, 2, part, 0)
        pl.when(m < HALF - NT)(lambda: i_copy(m).start())
        pl.when(m >= HALF - NT)(lambda: finish(m))
        return k

    lax.fori_loop(0, HALF, bins_in, 0)

    def ticks(n, k):
        tick_left(n)
        return k

    lax.fori_loop(0, 2 * HALF, ticks, 0)
    def left(zb, k):
        @pl.when(z < NZ - 1)
        def _():
            z_copy(zb, True).wait_send()

        @pl.when(z > 0)
        def _():
            z_copy(zb, False).wait_send()

        @pl.when(y > 0)
        def _():
            y_copy(zb, False).wait_send()

        @pl.when(y < ny - 1)
        def _():
            y_copy(zb, True).wait_send()

        c_copy(zb).wait_send()
        return k

    lax.fori_loop(0, NZ, left, 0)
    some = hb.at[pl.ds(0, NR - 1)]
    pltpu.make_async_copy(some, some, sh.at[0]).wait()

    def shown(m, k):
        i_copy(m).wait_send()
        return k

    lax.fori_loop(0, HALF - NT, shown, 0)


def local(field, bin_ids, table_color, table_opacity):
    cols = field.shape[2]
    out = jax.ShapeDtypeStruct((4, BR, cols), F32)
    vm = pl.BlockSpec(memory_space=pltpu.VMEM)
    hbm = pl.BlockSpec(memory_space=pltpu.HBM)
    dma = pltpu.SemaphoreType.DMA
    args = [
        pltpu.with_memory_space_constraint(a, pltpu.HBM)
        for a in (field, bin_ids, table_color, table_opacity)
    ]
    return pl.pallas_call(
        kernel,
        out_shape=(out, out),
        in_specs=[hbm] * 4,
        out_specs=(vm, vm),
        scratch_shapes=[
            pltpu.VMEM(table_color.shape, table_color.dtype),
            pltpu.VMEM(table_opacity.shape, table_opacity.dtype),
            pltpu.VMEM((NZ, NT + 2, NS + 4, BR + 16, 128), F32),
            pltpu.VMEM((NZ, NS, BR, cols), jnp.int32),
            pltpu.VMEM((NR, 2, NT, 8, 128), F32),
            pltpu.VMEM((NR, 2, NT, 8, 128), F32),
            pltpu.VMEM(field.shape, F32),
            pltpu.VMEM((NZ, NS, BR, cols), F32),
            pltpu.VMEM((NZ, NS, BR, cols), F32),
            pltpu.VMEM((HALF, 7, BR, 128), F32),
            pltpu.VMEM((NZ, NT, 7, BR, 128), F32),
            dma((3,)), dma((NZ,)), dma((HALF,)), dma((1,)), dma((NZ, 2)), dma((NZ, 2)), dma((NZ,)), dma((NZ, NT)),
            dma((2 * HALF,)), dma((1,)), dma((NZ, 2)), dma((NZ, 2)), dma((NZ,)), dma((HALF,)),
        ],
        compiler_params=pltpu.CompilerParams(
            collective_id=0, has_side_effects=True, vmem_limit_bytes=40 * 2**20),
    )(*args)


def solution(mesh):
    return jax.shard_map(
        local,
        mesh=mesh,
        in_specs=(P("depth", None, "tile"), P("depth", None, "tile"), P(), P()),
        out_specs=(P(None, "depth", "tile"), P(None, "depth", "tile")),
        check_vma=False,
    )
```

```python
import jax
import jax.numpy as jnp
from jax import lax
from jax.experimental import pallas as pl
from jax.experimental.pallas import tpu as pltpu
from jax.sharding import PartitionSpec as P

MESH = pl.DeviceIdType.MESH
F32 = jnp.float32
NZ, NX, NC = 4, 4, 2
NR = NX * NC
NS = 2 * NR
BR = 16
NT = 4
TOP = 8
HALF = NZ * NT


def kernel(
    field, bins, tcol_h, topa_h, front, back,
    tcol, topa, fb, bb, hb, hs, fv, ga, gl, stage, img,
    lsem, fsem, bsem, hsem, zsem, ysem, csem, isem, sx, sh, sz, sy, sc, si, ring, near,
):
    d = lax.axis_index("depth")
    y = lax.axis_index("tile")
    ny = lax.axis_size("tile")
    z = d // NR
    xc = d % NR
    x = xc // NC
    c = xc % NC

    load = pltpu.make_async_copy(field, fv, lsem.at[0])
    load.start()
    tload = [pltpu.make_async_copy(tcol_h, tcol, lsem.at[1]), pltpu.make_async_copy(topa_h, topa, lsem.at[2])]
    for cp in tload:
        cp.start()
    bar = pltpu.get_barrier_semaphore()

    def here(z_, x_, c_, y_):
        pl.semaphore_signal(bar, inc=1, device_id=((z_ * NX + x_) * NC + c_, y_), device_id_type=MESH)

    for p in range(1, NX):
        here(z, (x + p) % NX, 0, y)
    pl.when(c == 1)(lambda: here(z, x, 0, y))
    for p in range(1, NZ):
        here((z + p) % NZ, x, 1, y)
    for p in (1, ny - 1):
        here(z, x, 1, (y + p) % ny)

    @pl.when(y == 0)
    def _():
        fb[:, 0, 2:2 + NS, TOP:TOP + BR, :] = jnp.zeros((NZ, NS, BR, 128), F32)

    @pl.when(y == ny - 1)
    def _():
        fb[:, NT + 1, 2:2 + NS, TOP:TOP + BR, :] = jnp.zeros((NZ, NS, BR, 128), F32)

    @pl.when(z == 0)
    def _():
        fb[:, 1:NT + 1, 0:2, TOP:TOP + BR, :] = jnp.zeros((NZ, NT, 2, BR, 128), F32)

    @pl.when(z == NZ - 1)
    def _():
        fb[:, 1:NT + 1, NS + 2:NS + 4, TOP:TOP + BR, :] = jnp.zeros((NZ, NT, 2, BR, 128), F32)

    def tell(sem, c_):
        pl.semaphore_signal(sem, inc=1, device_id=((z * NX + x) * NC + c_, y), device_id_type=MESH)

    @pl.when(c == 0)
    def _():
        pl.semaphore_wait(bar, NR - 1)
        tell(ring, 1)

    @pl.when(c == 1)
    def _():
        pl.semaphore_wait(ring, 1)

    def rows_of(zb, q):
        return pl.ds(pl.multiple_of((zb * NX + q // NC) * BR * NC + q % NC * BR, BR), BR)

    def copy_x(src, dst, send, recv, q):
        return pltpu.make_async_remote_copy(
            src_ref=src, dst_ref=dst, send_sem=send, recv_sem=recv,
            device_id=(z * NR + q, y), device_id_type=MESH)

    def bin_tile(m):
        t = m // NT
        mixed = (t % 3 + 1) // 2
        off = mixed * (1 + 2 * (m % 2)) + (1 - mixed) * 2 * (1 - t // 3)
        return (z + off) % NZ, mixed * ((m - NT) // 2) + (1 - mixed) * (m % NT)

    def tick_refs(n, q):
        f_zb, f_j = n // NT, n % NT
        b_zb, b_j = bin_tile(n - HALF)
        f_cols = pl.ds(pl.multiple_of(128 * f_j, 128), 128)
        b_cols = pl.ds(pl.multiple_of(128 * b_j, 128), 128)
        return (
            (field.at[:, rows_of(f_zb, q), f_cols], fb.at[f_zb, f_j + 1, pl.ds(2 + 2 * xc, 2), pl.ds(TOP, BR), :]),
            (bins.at[:, rows_of(b_zb, q), b_cols], bb.at[b_zb, pl.ds(2 * xc, 2), :, b_cols]),
        )

    def send_tick(n, k=0):
        for kind in range(2):
            @pl.when(n // HALF == kind)
            def _():
                recv = bsem.at[n - HALF] if kind else fsem.at[n // NT]
                src, dst = tick_refs(n, xc)[kind]
                pltpu.make_async_copy(src, dst, recv).start()

                def one(p, k2):
                    q = (xc + p) % NR
                    src, dst = tick_refs(n, q)[kind]
                    copy_x(src, dst, sx.at[n], recv, q).start()
                    return k2

                lax.fori_loop(1, NR, one, 0)
        return k

    def tick_left(n):
        some = bb.at[0, pl.ds(0, NS - 2), :, pl.ds(0, 128)]
        pltpu.make_async_copy(some, some, sx.at[n]).wait()

    def send_h():
        pltpu.make_async_copy(hs.at[xc], hb.at[xc], hsem.at[0]).start()

        def one(p, k):
            q = (xc + p) % NR
            copy_x(hs.at[q], hb.at[xc], sh.at[0], hsem.at[0], q).start()
            return k

        lax.fori_loop(1, NR, one, 0)

    lax.fori_loop(0, NT, send_tick, 0)

    load.wait()
    total = NZ * NX * NC * BR
    for q in range(NR):
        for zb in range(NZ):
            r0 = (zb * NX + q // NC) * BR * NC + (BR * NC if q % NC else -2)
            for s in range(2):
                o = zb % 2 * 4 + s * 2
                for j in range(NT):
                    if 0 <= r0 < total:
                        hs[q, zb // 2, j, o:o + 2, :] = fv[s, r0:r0 + 2, 128 * j:128 * j + 128]
                    else:
                        hs[q, zb // 2, j, o:o + 2, :] = jnp.zeros((2, 128), F32)

    send_h()
    lax.fori_loop(NT, 2 * HALF, send_tick, 0)

    for cp in tload:
        cp.wait()
    tc = tcol[...].astype(F32)
    to_ = topa[...].astype(F32).reshape(1, -1) * (1.0 / 144.0)
    tabs = []
    for k in range(3):
        tabs.append([jnp.broadcast_to(tc[k:k + 1, 128 * h:128 * h + 128], (8, 128)) for h in range(2)])
    tabs.append([jnp.broadcast_to(to_[:, 128 * h:128 * h + 128], (8, 128)) for h in range(2)])

    def z_copy(zb, up):
        src = fb.at[zb, pl.ds(1, NT), pl.ds(NS if up else 2, 2), pl.ds(TOP, BR), :]
        dst = fb.at[zb, pl.ds(1, NT), pl.ds(0 if up else NS + 2, 2), pl.ds(TOP, BR), :]
        return pltpu.make_async_remote_copy(
            src_ref=src, dst_ref=dst, send_sem=sz.at[zb, int(up)], recv_sem=zsem.at[zb, int(up)],
            device_id=(d + (NR if up else -NR), y), device_id_type=MESH)

    def y_copy(zb, right):
        src = fb.at[zb, NT if right else 1, pl.ds(2, NS), pl.ds(TOP, BR), :]
        dst = fb.at[zb, 0 if right else NT + 1, pl.ds(2, NS), pl.ds(TOP, BR), :]
        return pltpu.make_async_remote_copy(
            src_ref=src, dst_ref=dst, send_sem=sy.at[zb, int(right)], recv_sem=ysem.at[zb, int(right)],
            device_id=(d, y + (1 if right else -1)), device_id_type=MESH)

    def c_copy(zb):
        src = fb.at[zb, pl.ds(1, NT), pl.ds(2, NS), pl.ds(pl.multiple_of(TOP + 8 * (1 - c), 8), 8), :]
        dst = fb.at[zb, pl.ds(1, NT), pl.ds(2, NS), pl.ds(pl.multiple_of((TOP + BR) * c, 8), 8), :]
        return pltpu.make_async_remote_copy(
            src_ref=src, dst_ref=dst, send_sem=sc.at[zb], recv_sem=csem.at[zb],
            device_id=(d + 1 - 2 * c, y), device_id_type=MESH)

    def pass_on(zb):
        own = fb.at[zb, pl.ds(1, NT), pl.ds(2, NS), pl.ds(TOP, BR), :]
        pltpu.make_async_copy(own, own, fsem.at[zb]).wait()

        @pl.when(z < NZ - 1)
        def _():
            z_copy(zb, True).start()

        @pl.when(z > 0)
        def _():
            z_copy(zb, False).start()

        @pl.when(y > 0)
        def _():
            y_copy(zb, False).start()

        @pl.when(y < ny - 1)
        def _():
            y_copy(zb, True).start()

        c_copy(zb).start()

    def rows_in(i, k, at):
        for zb in range(NZ):
            for s in range(2):
                a = zb % 2 * 4 + s * 2
                for j in range(NT):
                    fb[zb, j + 1, 2 + 2 * i + s, at:at + 2, :] = hb[i, zb // 2, j, a:a + 2, :]
        return k

    def all_rows_in():
        pltpu.make_async_copy(hb, hb, hsem.at[0]).wait()

        @pl.when(c == 0)
        def _():
            lax.fori_loop(0, NR, lambda i, k: rows_in(i, k, TOP - 2), 0)

        @pl.when(c == 1)
        def _():
            lax.fori_loop(0, NR, lambda i, k: rows_in(i, k, TOP + BR), 0)

    def halos(zb):
        @pl.when(z > 0)
        def _():
            z_copy(zb, True).wait_recv()

        @pl.when(z < NZ - 1)
        def _():
            z_copy(zb, False).wait_recv()

        @pl.when(y > 0)
        def _():
            y_copy(zb, True).wait_recv()

        @pl.when(y < ny - 1)
        def _():
            y_copy(zb, False).wait_recv()

        c_copy(zb).wait_recv()

    lane = lax.broadcasted_iota(jnp.int32, (8, 128), 1)
    kd, kr, kc = 0.7 * 0.48 / 12.0, 0.7 * 0.6 / 12.0, 0.7 * 0.64 / 12.0

    def gradients(zb, j, g):
        r = pl.multiple_of(TOP + 8 * g, 8)
        rows = pl.ds(pl.multiple_of(8 * g, 8), 8)
        lanes = pl.ds(pl.multiple_of(128 * j, 128), 128)
        win = [fb[zb, j + 1, s, pl.ds(r, 8), :] for s in range(4)]
        for s in range(NS):
            win.append(fb[zb, j + 1, s + 4, pl.ds(r, 8), :])
            v = win[s + 2]
            gd = 8.0 * (win[s + 3] - win[s + 1]) + (win[s] - win[s + 4])
            m2, m1, p1, p2 = [fb[zb, j + 1, s + 2, pl.ds(r + o, 8), :] for o in (-2, -1, 1, 2)]
            gr = 8.0 * (p1 - m1) + (m2 - p2)
            lt = fb[zb, j, s + 2, pl.ds(r, 8), :]
            rt = fb[zb, j + 2, s + 2, pl.ds(r, 8), :]
            l1 = pltpu.roll(jnp.where(lane == 127, lt, v), 1, 1)
            l2 = pltpu.roll(jnp.where(lane >= 126, lt, v), 2, 1)
            r1 = pltpu.roll(jnp.where(lane == 0, rt, v), 127, 1)
            r2 = pltpu.roll(jnp.where(lane < 2, rt, v), 126, 1)
            gc = 8.0 * (r1 - l1) + (l2 - r2)
            q = gd * gd + gr * gr + gc * gc
            inv = lax.rsqrt(q * (1.0 / 144.0) + 1.0)
            a = q * (inv * inv)
            ga[zb, s, rows, lanes] = a
            gl[zb, s, rows, lanes] = a * (0.3 + jnp.abs(kd * gd + kr * gr + kc * gc) * inv)

    def shade(zb, j, g, m):
        rows = pl.ds(pl.multiple_of(8 * g, 8), 8)
        lanes = pl.ds(pl.multiple_of(128 * j, 128), 128)
        fr = [jnp.zeros((8, 128), F32) for _ in range(3)]
        bk = [jnp.zeros((8, 128), F32) for _ in range(3)]
        tr = jnp.ones((8, 128), F32)
        for s in range(NS):
            ids = bb[zb, s, rows, lanes]
            low = ids & 127
            upper = ids >= 128
            look = [
                jnp.where(upper,
                          jnp.take_along_axis(hi, low, axis=1, mode="promise_in_bounds"),
                          jnp.take_along_axis(lo, low, axis=1, mode="promise_in_bounds"))
                for lo, hi in tabs
            ]
            keep = 1.0 - look[3] * ga[zb, s, rows, lanes]
            w = look[3] * gl[zb, s, rows, lanes]
            for k in range(3):
                col = look[k] * w
                fr[k] = fr[k] + tr * col
                bk[k] = bk[k] * keep + col
            tr = tr * keep
        for k, part in enumerate(fr + bk + [tr]):
            stage[m, k, rows, :] = part

    def i_copy(m):
        zb, j = bin_tile(m)
        return pltpu.make_async_remote_copy(
            src_ref=stage.at[m], dst_ref=img.at[z, j], send_sem=si.at[m], recv_sem=isem.at[z, j],
            device_id=(zb * NR + xc, y), device_id_type=MESH)

    def finish(m):
        j = m % NT
        img[z, j] = stage[m]
        for p in range(1, NZ):
            other = img.at[(z + p) % NZ, j]
            pltpu.make_async_copy(other, other, isem.at[(z + p) % NZ, j]).wait()
        lanes = pl.ds(pl.multiple_of(128 * j, 128), 128)
        ts = [img[s, j, 6] for s in range(NZ)]
        t = (ts[0] * ts[1]) * (ts[2] * ts[3])
        for n in range(3):
            acc = img[NZ - 1, j, n]
            for s in range(NZ - 2, -1, -1):
                acc = img[s, j, n] + ts[s] * acc
            front[n, :, lanes] = acc
            acc = img[0, j, 3 + n]
            for s in range(1, NZ):
                acc = img[s, j, 3 + n] + ts[s] * acc
            back[n, :, lanes] = acc
        front[3, :, lanes] = t
        back[3, :, lanes] = t

    def cells_in(n, k):
        pl.when(n < NZ)(lambda: pass_on(n))
        pl.when(n == 1)(all_rows_in)

        @pl.when(n > 0)
        def _():
            halos(n - 1)

            def part(h, k2):
                gradients(n - 1, h // 2, h % 2)
                return k2

            lax.fori_loop(0, 2 * NT, part, 0)
        return k

    @pl.when(c == 1)
    def _():
        pl.semaphore_wait(bar, (NZ - 1 + 2) * NC)
        tell(near, 0)

    @pl.when(c == 0)
    def _():
        pl.semaphore_wait(near, 1)

    lax.fori_loop(0, NZ + 1, cells_in, 0)

    def drain(m):
        @pl.when(m >= NT)
        def _():
            tick_left(2 * (m - NT))
            tick_left(2 * (m - NT) + 1)

        zb = m - 2 * NT

        @pl.when(jnp.logical_and(zb >= 0, zb < NZ))
        def _():
            @pl.when(z < NZ - 1)
            def _():
                z_copy(zb, True).wait_send()

            @pl.when(z > 0)
            def _():
                z_copy(zb, False).wait_send()

            @pl.when(y > 0)
            def _():
                y_copy(zb, False).wait_send()

            @pl.when(y < ny - 1)
            def _():
                y_copy(zb, True).wait_send()

            c_copy(zb).wait_send()

        @pl.when(m == 2 * NT)
        def _():
            some = hb.at[pl.ds(0, NR - 1)]
            pltpu.make_async_copy(some, some, sh.at[0]).wait()

        @pl.when(m >= HALF - NT)
        def _():
            for i in range(3):
                i_copy(3 * (m - HALF + NT) + i).wait_send()

    def bins_in(m, k):
        drain(m)
        zb, j = bin_tile(m)
        got = bb.at[zb, :, :, pl.ds(pl.multiple_of(128 * j, 128), 128)]
        pltpu.make_async_copy(got, got, bsem.at[m]).wait()

        def part(h, k2):
            shade(zb, j, h, m)
            return k2

        lax.fori_loop(0, 2, part, 0)
        pl.when(m < HALF - NT)(lambda: i_copy(m).start())
        pl.when(m >= HALF - NT)(lambda: finish(m))
        return k

    lax.fori_loop(0, HALF, bins_in, 0)

    for n in range(2 * HALF - 2 * NT, 2 * HALF):
        tick_left(n)


def local(field, bin_ids, table_color, table_opacity):
    cols = field.shape[2]
    out = jax.ShapeDtypeStruct((4, BR, cols), F32)
    vm = pl.BlockSpec(memory_space=pltpu.VMEM)
    hbm = pl.BlockSpec(memory_space=pltpu.HBM)
    dma = pltpu.SemaphoreType.DMA
    args = [
        pltpu.with_memory_space_constraint(a, pltpu.HBM)
        for a in (field, bin_ids, table_color, table_opacity)
    ]
    return pl.pallas_call(
        kernel,
        out_shape=(out, out),
        in_specs=[hbm] * 4,
        out_specs=(vm, vm),
        scratch_shapes=[
            pltpu.VMEM(table_color.shape, table_color.dtype),
            pltpu.VMEM(table_opacity.shape, table_opacity.dtype),
            pltpu.VMEM((NZ, NT + 2, NS + 4, BR + 16, 128), F32),
            pltpu.VMEM((NZ, NS, BR, cols), jnp.int32),
            pltpu.VMEM((NR, 2, NT, 8, 128), F32),
            pltpu.VMEM((NR, 2, NT, 8, 128), F32),
            pltpu.VMEM(field.shape, F32),
            pltpu.VMEM((NZ, NS, BR, cols), F32),
            pltpu.VMEM((NZ, NS, BR, cols), F32),
            pltpu.VMEM((HALF, 7, BR, 128), F32),
            pltpu.VMEM((NZ, NT, 7, BR, 128), F32),
            dma((3,)), dma((NZ,)), dma((HALF,)), dma((1,)), dma((NZ, 2)), dma((NZ, 2)), dma((NZ,)), dma((NZ, NT)),
            dma((2 * HALF,)), dma((1,)), dma((NZ, 2)), dma((NZ, 2)), dma((NZ,)), dma((HALF,)),
            pltpu.SemaphoreType.REGULAR, pltpu.SemaphoreType.REGULAR,
        ],
        compiler_params=pltpu.CompilerParams(
            collective_id=0, has_side_effects=True, vmem_limit_bytes=40 * 2**20),
    )(*args)


def solution(mesh):
    return jax.shard_map(
        local,
        mesh=mesh,
        in_specs=(P("depth", None, "tile"), P("depth", None, "tile"), P(), P()),
        out_specs=(P(None, "depth", "tile"), P(None, "depth", "tile")),
        check_vma=False,
    )
```

```python
import jax
import jax.numpy as jnp
from jax import lax
from jax.experimental import pallas as pl
from jax.experimental.pallas import tpu as pltpu
from jax.sharding import PartitionSpec as P

MESH = pl.DeviceIdType.MESH
F32 = jnp.float32
NZ, NX, NC = 4, 4, 2
NR = NX * NC
NS = 2 * NR
BR = 16
NT = 4
TOP = 8
HALF = NZ * NT


def kernel(
    field, bins, tcol_h, topa_h, front, back,
    tcol, topa, fb, bb, hb, hs, fv, ga, gl, stage, img,
    lsem, fsem, bsem, hsem, zsem, ysem, csem, isem, sx, sh, sz, sy, sc, si, ring, near,
):
    d = lax.axis_index("depth")
    y = lax.axis_index("tile")
    ny = lax.axis_size("tile")
    z = d // NR
    xc = d % NR
    x = xc // NC
    c = xc % NC

    load = pltpu.make_async_copy(field, fv, lsem.at[0])
    load.start()
    tload = [pltpu.make_async_copy(tcol_h, tcol, lsem.at[1]), pltpu.make_async_copy(topa_h, topa, lsem.at[2])]
    for cp in tload:
        cp.start()
    bar = pltpu.get_barrier_semaphore()

    def here(z_, x_, c_, y_):
        pl.semaphore_signal(bar, inc=1, device_id=((z_ * NX + x_) * NC + c_, y_), device_id_type=MESH)

    for p in range(1, NX):
        here(z, (x + p) % NX, 0, y)
    pl.when(c == 1)(lambda: here(z, x, 0, y))
    for p in range(1, NZ):
        here((z + p) % NZ, x, 1, y)
    for p in (1, ny - 1):
        here(z, x, 1, (y + p) % ny)

    @pl.when(y == 0)
    def _():
        fb[:, 0, 2:2 + NS, TOP:TOP + BR, :] = jnp.zeros((NZ, NS, BR, 128), F32)

    @pl.when(y == ny - 1)
    def _():
        fb[:, NT + 1, 2:2 + NS, TOP:TOP + BR, :] = jnp.zeros((NZ, NS, BR, 128), F32)

    @pl.when(z == 0)
    def _():
        fb[:, 1:NT + 1, 0:2, TOP:TOP + BR, :] = jnp.zeros((NZ, NT, 2, BR, 128), F32)

    @pl.when(z == NZ - 1)
    def _():
        fb[:, 1:NT + 1, NS + 2:NS + 4, TOP:TOP + BR, :] = jnp.zeros((NZ, NT, 2, BR, 128), F32)

    def tell(sem, c_):
        pl.semaphore_signal(sem, inc=1, device_id=((z * NX + x) * NC + c_, y), device_id_type=MESH)

    @pl.when(c == 0)
    def _():
        pl.semaphore_wait(bar, NR - 1)
        tell(ring, 1)

    @pl.when(c == 1)
    def _():
        pl.semaphore_wait(ring, 1)

    def rows_of(zb, q):
        return pl.ds(pl.multiple_of((zb * NX + q // NC) * BR * NC + q % NC * BR, BR), BR)

    def copy_x(src, dst, send, recv, q):
        return pltpu.make_async_remote_copy(
            src_ref=src, dst_ref=dst, send_sem=send, recv_sem=recv,
            device_id=(z * NR + q, y), device_id_type=MESH)

    def bin_tile(m):
        t = m // NT
        mixed = (t % 3 + 1) // 2
        off = mixed * (1 + 2 * (m % 2)) + (1 - mixed) * 2 * (1 - t // 3)
        return (z + off) % NZ, mixed * ((m - NT) // 2) + (1 - mixed) * (m % NT)

    def tick_refs(n, q):
        f_zb, f_j = n // NT, n % NT
        b_zb, b_j = bin_tile(n - HALF)
        f_cols = pl.ds(pl.multiple_of(128 * f_j, 128), 128)
        b_cols = pl.ds(pl.multiple_of(128 * b_j, 128), 128)
        return (
            (field.at[:, rows_of(f_zb, q), f_cols], fb.at[f_zb, f_j + 1, pl.ds(2 + 2 * xc, 2), pl.ds(TOP, BR), :]),
            (bins.at[:, rows_of(b_zb, q), b_cols], bb.at[b_zb, pl.ds(2 * xc, 2), :, b_cols]),
        )

    def send_tick(n, k=0):
        for kind in range(2):
            @pl.when(n // HALF == kind)
            def _():
                recv = bsem.at[n - HALF] if kind else fsem.at[n // NT]
                src, dst = tick_refs(n, xc)[kind]
                pltpu.make_async_copy(src, dst, recv).start()

                def one(p, k2):
                    q = (xc + p) % NR
                    src, dst = tick_refs(n, q)[kind]
                    copy_x(src, dst, sx.at[n], recv, q).start()
                    return k2

                lax.fori_loop(1, NR, one, 0)
        return k

    def tick_left(n):
        some = bb.at[0, pl.ds(0, NS - 2), :, pl.ds(0, 128)]
        pltpu.make_async_copy(some, some, sx.at[n]).wait()

    def send_h():
        pltpu.make_async_copy(hs.at[xc], hb.at[xc], hsem.at[0]).start()

        def one(p, k):
            q = (xc + p) % NR
            copy_x(hs.at[q], hb.at[xc], sh.at[0], hsem.at[0], q).start()
            return k

        lax.fori_loop(1, NR, one, 0)

    lax.fori_loop(0, NT, send_tick, 0)

    load.wait()
    total = NZ * NX * NC * BR
    for q in range(NR):
        for zb in range(NZ):
            r0 = (zb * NX + q // NC) * BR * NC + (BR * NC if q % NC else -2)
            for s in range(2):
                o = zb % 2 * 4 + s * 2
                for j in range(NT):
                    if 0 <= r0 < total:
                        hs[q, zb // 2, j, o:o + 2, :] = fv[s, r0:r0 + 2, 128 * j:128 * j + 128]
                    else:
                        hs[q, zb // 2, j, o:o + 2, :] = jnp.zeros((2, 128), F32)

    send_h()
    lax.fori_loop(NT, 2 * HALF, send_tick, 0)

    for cp in tload:
        cp.wait()
    tc = tcol[...].astype(F32)
    to_ = topa[...].astype(F32).reshape(1, -1) * (1.0 / 144.0)
    tabs = []
    for k in range(3):
        tabs.append([jnp.broadcast_to(tc[k:k + 1, 128 * h:128 * h + 128], (8, 128)) for h in range(2)])
    tabs.append([jnp.broadcast_to(to_[:, 128 * h:128 * h + 128], (8, 128)) for h in range(2)])

    def z_copy(zb, up):
        src = fb.at[zb, pl.ds(1, NT), pl.ds(NS if up else 2, 2), pl.ds(TOP, BR), :]
        dst = fb.at[zb, pl.ds(1, NT), pl.ds(0 if up else NS + 2, 2), pl.ds(TOP, BR), :]
        return pltpu.make_async_remote_copy(
            src_ref=src, dst_ref=dst, send_sem=sz.at[zb, int(up)], recv_sem=zsem.at[zb, int(up)],
            device_id=(d + (NR if up else -NR), y), device_id_type=MESH)

    def y_copy(zb, right):
        src = fb.at[zb, NT if right else 1, pl.ds(2, NS), pl.ds(TOP, BR), :]
        dst = fb.at[zb, 0 if right else NT + 1, pl.ds(2, NS), pl.ds(TOP, BR), :]
        return pltpu.make_async_remote_copy(
            src_ref=src, dst_ref=dst, send_sem=sy.at[zb, int(right)], recv_sem=ysem.at[zb, int(right)],
            device_id=(d, y + (1 if right else -1)), device_id_type=MESH)

    def c_copy(zb):
        src = fb.at[zb, pl.ds(1, NT), pl.ds(2, NS), pl.ds(pl.multiple_of(TOP + 8 * (1 - c), 8), 8), :]
        dst = fb.at[zb, pl.ds(1, NT), pl.ds(2, NS), pl.ds(pl.multiple_of((TOP + BR) * c, 8), 8), :]
        return pltpu.make_async_remote_copy(
            src_ref=src, dst_ref=dst, send_sem=sc.at[zb], recv_sem=csem.at[zb],
            device_id=(d + 1 - 2 * c, y), device_id_type=MESH)

    def pass_on(zb):
        own = fb.at[zb, pl.ds(1, NT), pl.ds(2, NS), pl.ds(TOP, BR), :]
        pltpu.make_async_copy(own, own, fsem.at[zb]).wait()

        @pl.when(z < NZ - 1)
        def _():
            z_copy(zb, True).start()

        @pl.when(z > 0)
        def _():
            z_copy(zb, False).start()

        @pl.when(y > 0)
        def _():
            y_copy(zb, False).start()

        @pl.when(y < ny - 1)
        def _():
            y_copy(zb, True).start()

        c_copy(zb).start()

    def rows_in(i, k, at):
        for zb in range(NZ):
            for s in range(2):
                a = zb % 2 * 4 + s * 2
                for j in range(NT):
                    fb[zb, j + 1, 2 + 2 * i + s, at:at + 2, :] = hb[i, zb // 2, j, a:a + 2, :]
        return k

    def all_rows_in():
        pltpu.make_async_copy(hb, hb, hsem.at[0]).wait()

        @pl.when(c == 0)
        def _():
            lax.fori_loop(0, NR, lambda i, k: rows_in(i, k, TOP - 2), 0)

        @pl.when(c == 1)
        def _():
            lax.fori_loop(0, NR, lambda i, k: rows_in(i, k, TOP + BR), 0)

    def halos(zb):
        @pl.when(z > 0)
        def _():
            z_copy(zb, True).wait_recv()

        @pl.when(z < NZ - 1)
        def _():
            z_copy(zb, False).wait_recv()

        @pl.when(y > 0)
        def _():
            y_copy(zb, True).wait_recv()

        @pl.when(y < ny - 1)
        def _():
            y_copy(zb, False).wait_recv()

        c_copy(zb).wait_recv()

    lane = lax.broadcasted_iota(jnp.int32, (8, 128), 1)
    kd, kr, kc = 0.7 * 0.48 / 12.0, 0.7 * 0.6 / 12.0, 0.7 * 0.64 / 12.0

    def gradients(zb, j, g):
        r = pl.multiple_of(TOP + 8 * g, 8)
        rows = pl.ds(pl.multiple_of(8 * g, 8), 8)
        lanes = pl.ds(pl.multiple_of(128 * j, 128), 128)
        win = [fb[zb, j + 1, s, pl.ds(r, 8), :] for s in range(4)]
        for s in range(NS):
            win.append(fb[zb, j + 1, s + 4, pl.ds(r, 8), :])
            v = win[s + 2]
            gd = 8.0 * (win[s + 3] - win[s + 1]) + (win[s] - win[s + 4])
            m2, m1, p1, p2 = [fb[zb, j + 1, s + 2, pl.ds(r + o, 8), :] for o in (-2, -1, 1, 2)]
            gr = 8.0 * (p1 - m1) + (m2 - p2)
            lt = fb[zb, j, s + 2, pl.ds(r, 8), :]
            rt = fb[zb, j + 2, s + 2, pl.ds(r, 8), :]
            l1 = pltpu.roll(jnp.where(lane == 127, lt, v), 1, 1)
            l2 = pltpu.roll(jnp.where(lane >= 126, lt, v), 2, 1)
            r1 = pltpu.roll(jnp.where(lane == 0, rt, v), 127, 1)
            r2 = pltpu.roll(jnp.where(lane < 2, rt, v), 126, 1)
            gc = 8.0 * (r1 - l1) + (l2 - r2)
            q = gd * gd + gr * gr + gc * gc
            inv = lax.rsqrt(q * (1.0 / 144.0) + 1.0)
            a = q * (inv * inv)
            ga[zb, s, rows, lanes] = a
            gl[zb, s, rows, lanes] = a * (0.3 + jnp.abs(kd * gd + kr * gr + kc * gc) * inv)

    def shade(zb, j, g, m):
        rows = pl.ds(pl.multiple_of(8 * g, 8), 8)
        lanes = pl.ds(pl.multiple_of(128 * j, 128), 128)
        fr = [jnp.zeros((8, 128), F32) for _ in range(3)]
        bk = [jnp.zeros((8, 128), F32) for _ in range(3)]
        tr = jnp.ones((8, 128), F32)
        for s in range(NS):
            ids = bb[zb, s, rows, lanes]
            low = ids & 127
            upper = ids >= 128
            look = [
                jnp.where(upper,
                          jnp.take_along_axis(hi, low, axis=1, mode="promise_in_bounds"),
                          jnp.take_along_axis(lo, low, axis=1, mode="promise_in_bounds"))
                for lo, hi in tabs
            ]
            keep = 1.0 - look[3] * ga[zb, s, rows, lanes]
            w = look[3] * gl[zb, s, rows, lanes]
            for k in range(3):
                col = look[k] * w
                fr[k] = fr[k] + tr * col
                bk[k] = bk[k] * keep + col
            tr = tr * keep
        for k, part in enumerate(fr + bk + [tr]):
            stage[m, k, rows, :] = part

    def i_copy(m):
        zb, j = bin_tile(m)
        return pltpu.make_async_remote_copy(
            src_ref=stage.at[m], dst_ref=img.at[z, j], send_sem=si.at[m], recv_sem=isem.at[z, j],
            device_id=(zb * NR + xc, y), device_id_type=MESH)

    def finish(m):
        j = m % NT
        img[z, j] = stage[m]
        for p in range(1, NZ):
            other = img.at[(z + p) % NZ, j]
            pltpu.make_async_copy(other, other, isem.at[(z + p) % NZ, j]).wait()
        lanes = pl.ds(pl.multiple_of(128 * j, 128), 128)
        ts = [img[s, j, 6] for s in range(NZ)]
        t = (ts[0] * ts[1]) * (ts[2] * ts[3])
        for n in range(3):
            acc = img[NZ - 1, j, n]
            for s in range(NZ - 2, 0, -1):
                acc = img[s, j, n] + ts[s] * acc
            front[0, n, :, lanes] = img[0, j, n]
            front[1, n, :, lanes] = ts[0] * acc
            acc = img[0, j, 3 + n]
            for s in range(1, NZ - 1):
                acc = img[s, j, 3 + n] + ts[s] * acc
            back[0, n, :, lanes] = img[NZ - 1, j, 3 + n]
            back[1, n, :, lanes] = ts[NZ - 1] * acc
        for part, value in ((0, jnp.zeros_like(t)), (1, t)):
            front[part, 3, :, lanes] = value
            back[part, 3, :, lanes] = value

    def cells_in(n, k):
        pl.when(n < NZ)(lambda: pass_on(n))
        pl.when(n == 1)(all_rows_in)

        @pl.when(n > 0)
        def _():
            halos(n - 1)

            def part(h, k2):
                gradients(n - 1, h // 2, h % 2)
                return k2

            lax.fori_loop(0, 2 * NT, part, 0)
        return k

    @pl.when(c == 1)
    def _():
        pl.semaphore_wait(bar, (NZ - 1 + 2) * NC)
        tell(near, 0)

    @pl.when(c == 0)
    def _():
        pl.semaphore_wait(near, 1)

    lax.fori_loop(0, NZ + 1, cells_in, 0)

    def drain(m):
        @pl.when(m >= NT)
        def _():
            tick_left(2 * (m - NT))
            tick_left(2 * (m - NT) + 1)

        zb = m - 2 * NT

        @pl.when(jnp.logical_and(zb >= 0, zb < NZ))
        def _():
            @pl.when(z < NZ - 1)
            def _():
                z_copy(zb, True).wait_send()

            @pl.when(z > 0)
            def _():
                z_copy(zb, False).wait_send()

            @pl.when(y > 0)
            def _():
                y_copy(zb, False).wait_send()

            @pl.when(y < ny - 1)
            def _():
                y_copy(zb, True).wait_send()

            c_copy(zb).wait_send()

        @pl.when(m == 2 * NT)
        def _():
            some = hb.at[pl.ds(0, NR - 1)]
            pltpu.make_async_copy(some, some, sh.at[0]).wait()

        @pl.when(m >= HALF - NT)
        def _():
            for i in range(3):
                i_copy(3 * (m - HALF + NT) + i).wait_send()

    def bins_in(m, k):
        drain(m)
        zb, j = bin_tile(m)
        got = bb.at[zb, :, :, pl.ds(pl.multiple_of(128 * j, 128), 128)]
        pltpu.make_async_copy(got, got, bsem.at[m]).wait()

        def part(h, k2):
            shade(zb, j, h, m)
            return k2

        lax.fori_loop(0, 2, part, 0)
        pl.when(m < HALF - NT)(lambda: i_copy(m).start())
        pl.when(m >= HALF - NT)(lambda: finish(m))
        return k

    lax.fori_loop(0, HALF, bins_in, 0)

    for n in range(2 * HALF - 2 * NT, 2 * HALF):
        tick_left(n)


def local(field, bin_ids, table_color, table_opacity):
    cols = field.shape[2]
    out = jax.ShapeDtypeStruct((2, 4, BR, cols), F32)
    vm = pl.BlockSpec(memory_space=pltpu.VMEM)
    hbm = pl.BlockSpec(memory_space=pltpu.HBM)
    dma = pltpu.SemaphoreType.DMA
    args = [
        pltpu.with_memory_space_constraint(a, pltpu.HBM)
        for a in (field, bin_ids, table_color, table_opacity)
    ]
    front, back = pl.pallas_call(
        kernel,
        out_shape=(out, out),
        in_specs=[hbm] * 4,
        out_specs=(vm, vm),
        scratch_shapes=[
            pltpu.VMEM(table_color.shape, table_color.dtype),
            pltpu.VMEM(table_opacity.shape, table_opacity.dtype),
            pltpu.VMEM((NZ, NT + 2, NS + 4, BR + 16, 128), F32),
            pltpu.VMEM((NZ, NS, BR, cols), jnp.int32),
            pltpu.VMEM((NR, 2, NT, 8, 128), F32),
            pltpu.VMEM((NR, 2, NT, 8, 128), F32),
            pltpu.VMEM(field.shape, F32),
            pltpu.VMEM((NZ, NS, BR, cols), F32),
            pltpu.VMEM((NZ, NS, BR, cols), F32),
            pltpu.VMEM((HALF, 7, BR, 128), F32),
            pltpu.VMEM((NZ, NT, 7, BR, 128), F32),
            dma((3,)), dma((NZ,)), dma((HALF,)), dma((1,)), dma((NZ, 2)), dma((NZ, 2)), dma((NZ,)), dma((NZ, NT)),
            dma((2 * HALF,)), dma((1,)), dma((NZ, 2)), dma((NZ, 2)), dma((NZ,)), dma((HALF,)),
            pltpu.SemaphoreType.REGULAR, pltpu.SemaphoreType.REGULAR,
        ],
        compiler_params=pltpu.CompilerParams(
            collective_id=0, has_side_effects=True, vmem_limit_bytes=40 * 2**20),
    )(*args)
    return front[0] + front[1], back[0] + back[1]


def solution(mesh):
    return jax.shard_map(
        local,
        mesh=mesh,
        in_specs=(P("depth", None, "tile"), P("depth", None, "tile"), P(), P()),
        out_specs=(P(None, "depth", "tile"), P(None, "depth", "tile")),
        check_vma=False,
    )
```

```python
import jax
import jax.numpy as jnp
from jax import lax
from jax.experimental import pallas as pl
from jax.experimental.pallas import tpu as pltpu
from jax.sharding import PartitionSpec as P

MESH = pl.DeviceIdType.MESH
F32 = jnp.float32
NZ, NX, NC = 4, 4, 2
NR = NX * NC
NS = 2 * NR
BR = 16
NT = 4
TOP = 8
HALF = NZ * NT


def kernel(
    field, bins, tcol_h, topa_h, front, back,
    tcol, topa, fb, bb, hb, hs, hp, ho, fv, ga, gl, stage, img,
    lsem, fsem, bsem, hsem, zsem, ysem, csem, isem, sx, sh, sz, sy, sc, si, osem, so, ring, near,
):
    d = lax.axis_index("depth")
    y = lax.axis_index("tile")
    ny = lax.axis_size("tile")
    z = d // NR
    xc = d % NR
    x = xc // NC
    c = xc % NC

    load = pltpu.make_async_copy(field, fv, lsem.at[0])
    load.start()
    tload = [pltpu.make_async_copy(tcol_h, tcol, lsem.at[1]), pltpu.make_async_copy(topa_h, topa, lsem.at[2])]
    for cp in tload:
        cp.start()
    bar = pltpu.get_barrier_semaphore()

    def here(z_, x_, c_, y_):
        pl.semaphore_signal(bar, inc=1, device_id=((z_ * NX + x_) * NC + c_, y_), device_id_type=MESH)

    for p in range(1, NX):
        here(z, (x + p) % NX, 0, y)
    pl.when(c == 1)(lambda: here(z, x, 0, y))
    for p in range(1, NZ):
        here((z + p) % NZ, x, 1, y)
    for p in (1, ny - 1):
        here(z, x, 1, (y + p) % ny)

    @pl.when(y == 0)
    def _():
        fb[:, 0, 2:2 + NS, TOP:TOP + BR, :] = jnp.zeros((NZ, NS, BR, 128), F32)

    @pl.when(y == ny - 1)
    def _():
        fb[:, NT + 1, 2:2 + NS, TOP:TOP + BR, :] = jnp.zeros((NZ, NS, BR, 128), F32)

    @pl.when(z == 0)
    def _():
        fb[:, 1:NT + 1, 0:2, TOP:TOP + BR, :] = jnp.zeros((NZ, NT, 2, BR, 128), F32)

    @pl.when(z == NZ - 1)
    def _():
        fb[:, 1:NT + 1, NS + 2:NS + 4, TOP:TOP + BR, :] = jnp.zeros((NZ, NT, 2, BR, 128), F32)

    def tell(sem, c_):
        pl.semaphore_signal(sem, inc=1, device_id=((z * NX + x) * NC + c_, y), device_id_type=MESH)

    @pl.when(c == 0)
    def _():
        pl.semaphore_wait(bar, NR - 1)
        tell(ring, 1)

    @pl.when(c == 1)
    def _():
        pl.semaphore_wait(ring, 1)

    def rows_of(zb, q):
        return pl.ds(pl.multiple_of((zb * NX + q // NC) * BR * NC + q % NC * BR, BR), BR)

    def copy_x(src, dst, send, recv, q):
        return pltpu.make_async_remote_copy(
            src_ref=src, dst_ref=dst, send_sem=send, recv_sem=recv,
            device_id=(z * NR + q, y), device_id_type=MESH)

    def bin_tile(m):
        t = m // NT
        mixed = (t % 3 + 1) // 2
        off = mixed * (1 + 2 * (m % 2)) + (1 - mixed) * 2 * (1 - t // 3)
        return (z + off) % NZ, mixed * ((m - NT) // 2) + (1 - mixed) * (m % NT)

    def tick_refs(n, q):
        f_zb, f_j = n // NT, n % NT
        b_zb, b_j = bin_tile(n - HALF)
        f_cols = pl.ds(pl.multiple_of(128 * f_j, 128), 128)
        b_cols = pl.ds(pl.multiple_of(128 * b_j, 128), 128)
        return (
            (field.at[:, rows_of(f_zb, q), f_cols], fb.at[f_zb, f_j + 1, pl.ds(2 + 2 * xc, 2), pl.ds(TOP, BR), :]),
            (bins.at[:, rows_of(b_zb, q), b_cols], bb.at[b_zb, pl.ds(2 * xc, 2), :, b_cols]),
        )

    def send_tick(n, k=0):
        for kind in range(2):
            @pl.when(n // HALF == kind)
            def _():
                recv = bsem.at[n - HALF] if kind else fsem.at[n // NT]
                src, dst = tick_refs(n, xc)[kind]
                pltpu.make_async_copy(src, dst, recv).start()

                def one(p, k2):
                    q = (xc + p) % NR
                    src, dst = tick_refs(n, q)[kind]
                    copy_x(src, dst, sx.at[n], recv, q).start()
                    return k2

                lax.fori_loop(1, NR, one, 0)
        return k

    def tick_left(n):
        some = bb.at[0, pl.ds(0, NS - 2), :, pl.ds(0, 128)]
        pltpu.make_async_copy(some, some, sx.at[n]).wait()

    def send_h():
        pltpu.make_async_copy(hs.at[xc], hb.at[xc], hsem.at[0]).start()

        def one(p, k):
            q = (xc + p) % NR

            @pl.when(q // NC != (x + 2) % NX)
            def _():
                copy_x(hs.at[q], hb.at[xc], sh.at[0], hsem.at[0], q).start()
            return k

        lax.fori_loop(1, NR, one, 0)

    lax.fori_loop(0, NT, send_tick, 0)

    load.wait()
    total = NZ * NX * NC * BR
    for q in range(NR):
        for zb in range(NZ):
            r0 = (zb * NX + q // NC) * BR * NC + (BR * NC if q % NC else -2)
            for s in range(2):
                o = zb % 2 * 4 + s * 2
                for j in range(NT):
                    if 0 <= r0 < total:
                        hs[q, zb // 2, j, o:o + 2, :] = fv[s, r0:r0 + 2, 128 * j:128 * j + 128]
                    else:
                        hs[q, zb // 2, j, o:o + 2, :] = jnp.zeros((2, 128), F32)

    send_h()
    lax.fori_loop(NT, HALF, send_tick, 0)

    for cp in tload:
        cp.wait()
    tc = tcol[...].astype(F32)
    to_ = topa[...].astype(F32).reshape(1, -1) * (1.0 / 144.0)
    tabs = []
    for k in range(3):
        tabs.append([jnp.broadcast_to(tc[k:k + 1, 128 * h:128 * h + 128], (8, 128)) for h in range(2)])
    tabs.append([jnp.broadcast_to(to_[:, 128 * h:128 * h + 128], (8, 128)) for h in range(2)])

    def z_copy(zb, up):
        src = fb.at[zb, pl.ds(1, NT), pl.ds(NS if up else 2, 2), pl.ds(TOP, BR), :]
        dst = fb.at[zb, pl.ds(1, NT), pl.ds(0 if up else NS + 2, 2), pl.ds(TOP, BR), :]
        return pltpu.make_async_remote_copy(
            src_ref=src, dst_ref=dst, send_sem=sz.at[zb, int(up)], recv_sem=zsem.at[zb, int(up)],
            device_id=(d + (NR if up else -NR), y), device_id_type=MESH)

    def y_copy(zb, right):
        src = fb.at[zb, NT if right else 1, pl.ds(2, NS), pl.ds(TOP, BR), :]
        dst = fb.at[zb, 0 if right else NT + 1, pl.ds(2, NS), pl.ds(TOP, BR), :]
        return pltpu.make_async_remote_copy(
            src_ref=src, dst_ref=dst, send_sem=sy.at[zb, int(right)], recv_sem=ysem.at[zb, int(right)],
            device_id=(d, y + (1 if right else -1)), device_id_type=MESH)

    def c_copy(zb):
        src = fb.at[zb, pl.ds(1, NT), pl.ds(2, NS), pl.ds(pl.multiple_of(TOP + 8 * (1 - c), 8), 8), :]
        dst = fb.at[zb, pl.ds(1, NT), pl.ds(2, NS), pl.ds(pl.multiple_of((TOP + BR) * c, 8), 8), :]
        return pltpu.make_async_remote_copy(
            src_ref=src, dst_ref=dst, send_sem=sc.at[zb], recv_sem=csem.at[zb],
            device_id=(d + 1 - 2 * c, y), device_id_type=MESH)

    def pass_on(zb):
        own = fb.at[zb, pl.ds(1, NT), pl.ds(2, NS), pl.ds(TOP, BR), :]
        pltpu.make_async_copy(own, own, fsem.at[zb]).wait()

        @pl.when(z < NZ - 1)
        def _():
            z_copy(zb, True).start()

        @pl.when(z > 0)
        def _():
            z_copy(zb, False).start()

        @pl.when(y > 0)
        def _():
            y_copy(zb, False).start()

        @pl.when(y < ny - 1)
        def _():
            y_copy(zb, True).start()

        c_copy(zb).start()

    def rows_in(i, k, at):
        @pl.when(i // NC != (x + 2) % NX)
        def _():
            for zb in range(NZ):
                for s in range(2):
                    a = zb % 2 * 4 + s * 2
                    for j in range(NT):
                        fb[zb, j + 1, 2 + 2 * i + s, at:at + 2, :] = hb[i, zb // 2, j, a:a + 2, :]
        return k

    to_x = x + 2 * c - 1

    def o_copy(zb):
        to_b = zb + (to_x + NX) // NX - 1
        return pltpu.make_async_remote_copy(
            src_ref=hp.at[zb], dst_ref=ho.at[to_b], send_sem=so.at[zb], recv_sem=osem.at[to_b],
            device_id=((z * NX + (to_x + NX) % NX) * NC + 1 - c, y), device_id_type=MESH)

    def o_goes(zb):
        to_b = zb + (to_x + NX) // NX - 1
        return jnp.logical_and(to_b >= 0, to_b < NZ)

    def o_send(zb):
        for core, at in ((0, TOP), (1, TOP + BR - 2)):
            @pl.when(c == core)
            def _():
                for i in range(4):
                    s = 2 + 2 * NC * ((to_x + 2 + NX) % NX) + i
                    for j in range(NT):
                        hp[zb, j, 2 * i:2 * i + 2, :] = fb[zb, j + 1, s, at:at + 2, :]

        pl.when(o_goes(zb))(lambda: o_copy(zb).start())

    def o_in(zb):
        edge = (1 - c) * (x * NZ + zb) + c * ((NX - 1 - x) * NZ + NZ - 1 - zb) == 0

        @pl.when(edge)
        def _():
            ho[zb] = jnp.zeros((NT, 8, 128), F32)

        @pl.when(jnp.logical_not(edge))
        def _():
            got = ho.at[zb]
            pltpu.make_async_copy(got, got, osem.at[zb]).wait()

        for core, at in ((0, TOP - 2), (1, TOP + BR)):
            @pl.when(c == core)
            def _():
                for i in range(4):
                    s = 2 + 2 * NC * ((x + 2) % NX) + i
                    for j in range(NT):
                        fb[zb, j + 1, s, at:at + 2, :] = ho[zb, j, 2 * i:2 * i + 2, :]

    def all_rows_in():
        near_by = hb.at[pl.ds(0, NR - NC)]
        pltpu.make_async_copy(near_by, near_by, hsem.at[0]).wait()

        @pl.when(c == 0)
        def _():
            lax.fori_loop(0, NR, lambda i, k: rows_in(i, k, TOP - 2), 0)

        @pl.when(c == 1)
        def _():
            lax.fori_loop(0, NR, lambda i, k: rows_in(i, k, TOP + BR), 0)

    def halos(zb):
        @pl.when(z > 0)
        def _():
            z_copy(zb, True).wait_recv()

        @pl.when(z < NZ - 1)
        def _():
            z_copy(zb, False).wait_recv()

        @pl.when(y > 0)
        def _():
            y_copy(zb, True).wait_recv()

        @pl.when(y < ny - 1)
        def _():
            y_copy(zb, False).wait_recv()

        c_copy(zb).wait_recv()

    lane = lax.broadcasted_iota(jnp.int32, (8, 128), 1)
    kd, kr, kc = 0.7 * 0.48 / 12.0, 0.7 * 0.6 / 12.0, 0.7 * 0.64 / 12.0

    def gradients(zb, j, g):
        r = pl.multiple_of(TOP + 8 * g, 8)
        rows = pl.ds(pl.multiple_of(8 * g, 8), 8)
        lanes = pl.ds(pl.multiple_of(128 * j, 128), 128)
        win = [fb[zb, j + 1, s, pl.ds(r, 8), :] for s in range(4)]
        for s in range(NS):
            win.append(fb[zb, j + 1, s + 4, pl.ds(r, 8), :])
            v = win[s + 2]
            gd = 8.0 * (win[s + 3] - win[s + 1]) + (win[s] - win[s + 4])
            m2, m1, p1, p2 = [fb[zb, j + 1, s + 2, pl.ds(r + o, 8), :] for o in (-2, -1, 1, 2)]
            gr = 8.0 * (p1 - m1) + (m2 - p2)
            lt = fb[zb, j, s + 2, pl.ds(r, 8), :]
            rt = fb[zb, j + 2, s + 2, pl.ds(r, 8), :]
            l1 = pltpu.roll(jnp.where(lane == 127, lt, v), 1, 1)
            l2 = pltpu.roll(jnp.where(lane >= 126, lt, v), 2, 1)
            r1 = pltpu.roll(jnp.where(lane == 0, rt, v), 127, 1)
            r2 = pltpu.roll(jnp.where(lane < 2, rt, v), 126, 1)
            gc = 8.0 * (r1 - l1) + (l2 - r2)
            q = gd * gd + gr * gr + gc * gc
            inv = lax.rsqrt(q * (1.0 / 144.0) + 1.0)
            a = q * (inv * inv)
            ga[zb, s, rows, lanes] = a
            gl[zb, s, rows, lanes] = a * (0.3 + jnp.abs(kd * gd + kr * gr + kc * gc) * inv)

    def shade(zb, j, g, m):
        rows = pl.ds(pl.multiple_of(8 * g, 8), 8)
        lanes = pl.ds(pl.multiple_of(128 * j, 128), 128)
        fr = [jnp.zeros((8, 128), F32) for _ in range(3)]
        bk = [jnp.zeros((8, 128), F32) for _ in range(3)]
        tr = jnp.ones((8, 128), F32)
        for s in range(NS):
            ids = bb[zb, s, rows, lanes]
            low = ids & 127
            upper = ids >= 128
            look = [
                jnp.where(upper,
                          jnp.take_along_axis(hi, low, axis=1, mode="promise_in_bounds"),
                          jnp.take_along_axis(lo, low, axis=1, mode="promise_in_bounds"))
                for lo, hi in tabs
            ]
            keep = 1.0 - look[3] * ga[zb, s, rows, lanes]
            w = look[3] * gl[zb, s, rows, lanes]
            for k in range(3):
                col = look[k] * w
                fr[k] = fr[k] + tr * col
                bk[k] = bk[k] * keep + col
            tr = tr * keep
        for k, part in enumerate(fr + bk + [tr]):
            stage[m, k, rows, :] = part

    def i_copy(m):
        zb, j = bin_tile(m)
        return pltpu.make_async_remote_copy(
            src_ref=stage.at[m], dst_ref=img.at[z, j], send_sem=si.at[m], recv_sem=isem.at[z, j],
            device_id=(zb * NR + xc, y), device_id_type=MESH)

    def finish(m):
        j = m % NT
        img[z, j] = stage[m]
        for p in range(1, NZ):
            other = img.at[(z + p) % NZ, j]
            pltpu.make_async_copy(other, other, isem.at[(z + p) % NZ, j]).wait()
        lanes = pl.ds(pl.multiple_of(128 * j, 128), 128)
        ts = [img[s, j, 6] for s in range(NZ)]
        t = (ts[0] * ts[1]) * (ts[2] * ts[3])
        for n in range(3):
            acc = img[NZ - 1, j, n]
            for s in range(NZ - 2, 0, -1):
                acc = img[s, j, n] + ts[s] * acc
            front[0, n, :, lanes] = img[0, j, n]
            front[1, n, :, lanes] = ts[0] * acc
            acc = img[0, j, 3 + n]
            for s in range(1, NZ - 1):
                acc = img[s, j, 3 + n] + ts[s] * acc
            back[0, n, :, lanes] = img[NZ - 1, j, 3 + n]
            back[1, n, :, lanes] = ts[NZ - 1] * acc
        for part, value in ((0, jnp.zeros_like(t)), (1, t)):
            front[part, 3, :, lanes] = value
            back[part, 3, :, lanes] = value

    def cells_in(n, k):
        pass_on(n)
        o_send(n)
        pl.when(n == 1)(all_rows_in)

        @pl.when(n == NZ - 2)
        def _():
            lax.fori_loop(HALF, HALF + NT, send_tick, 0)

        @pl.when(n == NZ - 1)
        def _():
            lax.fori_loop(HALF + NT, 2 * HALF, send_tick, 0)

        return k

    def shape(n, k):
        halos(n)
        o_in(n)

        def part(h, k2):
            gradients(n, h // 2, h % 2)
            return k2

        lax.fori_loop(0, 2 * NT, part, 0)
        return k

    @pl.when(c == 1)
    def _():
        pl.semaphore_wait(bar, (NZ - 1 + 2) * NC)
        tell(near, 0)

    @pl.when(c == 0)
    def _():
        pl.semaphore_wait(near, 1)

    lax.fori_loop(0, NZ, cells_in, 0)
    lax.fori_loop(0, NZ, shape, 0)

    def drain(m):
        @pl.when(m >= NT)
        def _():
            tick_left(2 * (m - NT))
            tick_left(2 * (m - NT) + 1)

        zb = m - 2 * NT

        @pl.when(jnp.logical_and(zb >= 0, zb < NZ))
        def _():
            @pl.when(z < NZ - 1)
            def _():
                z_copy(zb, True).wait_send()

            @pl.when(z > 0)
            def _():
                z_copy(zb, False).wait_send()

            @pl.when(y > 0)
            def _():
                y_copy(zb, False).wait_send()

            @pl.when(y < ny - 1)
            def _():
                y_copy(zb, True).wait_send()

            c_copy(zb).wait_send()
            pl.when(o_goes(zb))(lambda: o_copy(zb).wait_send())

        @pl.when(m == 2 * NT)
        def _():
            some = hb.at[pl.ds(0, NR - NC - 1)]
            pltpu.make_async_copy(some, some, sh.at[0]).wait()

        @pl.when(m >= HALF - NT)
        def _():
            for i in range(3):
                i_copy(3 * (m - HALF + NT) + i).wait_send()

    def bins_in(m, k):
        drain(m)
        zb, j = bin_tile(m)
        got = bb.at[zb, :, :, pl.ds(pl.multiple_of(128 * j, 128), 128)]
        pltpu.make_async_copy(got, got, bsem.at[m]).wait()

        def part(h, k2):
            shade(zb, j, h, m)
            return k2

        lax.fori_loop(0, 2, part, 0)
        pl.when(m < HALF - NT)(lambda: i_copy(m).start())
        pl.when(m >= HALF - NT)(lambda: finish(m))
        return k

    lax.fori_loop(0, HALF, bins_in, 0)

    for n in range(2 * HALF - 2 * NT, 2 * HALF):
        tick_left(n)


def local(field, bin_ids, table_color, table_opacity):
    cols = field.shape[2]
    out = jax.ShapeDtypeStruct((2, 4, BR, cols), F32)
    vm = pl.BlockSpec(memory_space=pltpu.VMEM)
    hbm = pl.BlockSpec(memory_space=pltpu.HBM)
    dma = pltpu.SemaphoreType.DMA
    args = [
        pltpu.with_memory_space_constraint(a, pltpu.HBM)
        for a in (field, bin_ids, table_color, table_opacity)
    ]
    front, back = pl.pallas_call(
        kernel,
        out_shape=(out, out),
        in_specs=[hbm] * 4,
        out_specs=(vm, vm),
        scratch_shapes=[
            pltpu.VMEM(table_color.shape, table_color.dtype),
            pltpu.VMEM(table_opacity.shape, table_opacity.dtype),
            pltpu.VMEM((NZ, NT + 2, NS + 4, BR + 16, 128), F32),
            pltpu.VMEM((NZ, NS, BR, cols), jnp.int32),
            pltpu.VMEM((NR, 2, NT, 8, 128), F32),
            pltpu.VMEM((NR, 2, NT, 8, 128), F32),
            pltpu.VMEM((NZ, NT, 8, 128), F32),
            pltpu.VMEM((NZ, NT, 8, 128), F32),
            pltpu.VMEM(field.shape, F32),
            pltpu.VMEM((NZ, NS, BR, cols), F32),
            pltpu.VMEM((NZ, NS, BR, cols), F32),
            pltpu.VMEM((HALF, 7, BR, 128), F32),
            pltpu.VMEM((NZ, NT, 7, BR, 128), F32),
            dma((3,)), dma((NZ,)), dma((HALF,)), dma((1,)), dma((NZ, 2)), dma((NZ, 2)), dma((NZ,)), dma((NZ, NT)),
            dma((2 * HALF,)), dma((1,)), dma((NZ, 2)), dma((NZ, 2)), dma((NZ,)), dma((HALF,)),
            dma((NZ,)), dma((NZ,)), pltpu.SemaphoreType.REGULAR, pltpu.SemaphoreType.REGULAR,
        ],
        compiler_params=pltpu.CompilerParams(
            collective_id=0, has_side_effects=True, vmem_limit_bytes=40 * 2**20),
    )(*args)
    return front[0] + front[1], back[0] + back[1]


def solution(mesh):
    return jax.shard_map(
        local,
        mesh=mesh,
        in_specs=(P("depth", None, "tile"), P("depth", None, "tile"), P(), P()),
        out_specs=(P(None, "depth", "tile"), P(None, "depth", "tile")),
        check_vma=False,
    )
```

```python
import jax
import jax.numpy as jnp
from jax import lax
from jax.experimental import pallas as pl
from jax.experimental.pallas import tpu as pltpu
from jax.sharding import PartitionSpec as P

MESH = pl.DeviceIdType.MESH
F32 = jnp.float32
NZ, NX, NC = 4, 4, 2
NR = NX * NC
NS = 2 * NR
BR = 16
NT = 4
TOP = 8
HALF = NZ * NT


def kernel(
    field, bins, tcol_h, topa_h, front, back,
    tcol, topa, fb, bb, hb, hs, hp, ho, fv, ga, gl, stage, img,
    lsem, fsem, bsem, hsem, zsem, ysem, csem, isem, sx, sh, sz, sy, sc, si, osem, so, ring, near,
):
    d = lax.axis_index("depth")
    y = lax.axis_index("tile")
    ny = lax.axis_size("tile")
    z = d // NR
    xc = d % NR
    x = xc // NC
    c = xc % NC

    load = pltpu.make_async_copy(field, fv, lsem.at[0])
    load.start()
    tload = [pltpu.make_async_copy(tcol_h, tcol, lsem.at[1]), pltpu.make_async_copy(topa_h, topa, lsem.at[2])]
    for cp in tload:
        cp.start()
    bar = pltpu.get_barrier_semaphore()

    def here(z_, x_, c_, y_):
        pl.semaphore_signal(bar, inc=1, device_id=((z_ * NX + x_) * NC + c_, y_), device_id_type=MESH)

    for p in range(1, NX):
        here(z, (x + p) % NX, 0, y)
    pl.when(c == 1)(lambda: here(z, x, 0, y))
    for p in range(1, NZ):
        here((z + p) % NZ, x, 1, y)
    for p in (1, ny - 1):
        here(z, x, 1, (y + p) % ny)

    @pl.when(y == 0)
    def _():
        fb[:, 0, 2:2 + NS, TOP:TOP + BR, :] = jnp.zeros((NZ, NS, BR, 128), F32)

    @pl.when(y == ny - 1)
    def _():
        fb[:, NT + 1, 2:2 + NS, TOP:TOP + BR, :] = jnp.zeros((NZ, NS, BR, 128), F32)

    @pl.when(z == 0)
    def _():
        fb[:, 1:NT + 1, 0:2, TOP:TOP + BR, :] = jnp.zeros((NZ, NT, 2, BR, 128), F32)

    @pl.when(z == NZ - 1)
    def _():
        fb[:, 1:NT + 1, NS + 2:NS + 4, TOP:TOP + BR, :] = jnp.zeros((NZ, NT, 2, BR, 128), F32)

    def tell(sem, c_):
        pl.semaphore_signal(sem, inc=1, device_id=((z * NX + x) * NC + c_, y), device_id_type=MESH)

    @pl.when(c == 0)
    def _():
        pl.semaphore_wait(bar, NR - 1)
        tell(ring, 1)

    @pl.when(c == 1)
    def _():
        pl.semaphore_wait(ring, 1)

    def rows_of(zb, q):
        return pl.ds(pl.multiple_of((zb * NX + q // NC) * BR * NC + q % NC * BR, BR), BR)

    def copy_x(src, dst, send, recv, q):
        return pltpu.make_async_remote_copy(
            src_ref=src, dst_ref=dst, send_sem=send, recv_sem=recv,
            device_id=(z * NR + q, y), device_id_type=MESH)

    def bin_tile(m):
        t = m // NT
        mixed = (t % 3 + 1) // 2
        off = mixed * (1 + 2 * (m % 2)) + (1 - mixed) * 2 * (1 - t // 3)
        return (z + off) % NZ, mixed * ((m - NT) // 2) + (1 - mixed) * (m % NT)

    def tick_refs(n, q):
        f_zb, f_j = n // NT, n % NT
        b_zb, b_j = bin_tile(n - HALF)
        f_cols = pl.ds(pl.multiple_of(128 * f_j, 128), 128)
        b_cols = pl.ds(pl.multiple_of(128 * b_j, 128), 128)
        return (
            (field.at[:, rows_of(f_zb, q), f_cols], fb.at[f_zb, f_j + 1, pl.ds(2 + 2 * xc, 2), pl.ds(TOP, BR), :]),
            (bins.at[:, rows_of(b_zb, q), b_cols], bb.at[b_zb, pl.ds(2 * xc, 2), :, b_cols]),
        )

    def send_tick(n, k=0):
        for kind in range(2):
            @pl.when(n // HALF == kind)
            def _():
                recv = bsem.at[n - HALF] if kind else fsem.at[n // NT]
                src, dst = tick_refs(n, xc)[kind]
                pltpu.make_async_copy(src, dst, recv).start()

                def one(p, k2):
                    q = (xc + p) % NR
                    src, dst = tick_refs(n, q)[kind]
                    copy_x(src, dst, sx.at[kind], recv, q).start()
                    return k2

                lax.fori_loop(1, NR, one, 0)
        return k

    def ticks_left(kind):
        some = bb.at[:, pl.ds(0, NS - 2)]
        pltpu.make_async_copy(some, some, sx.at[kind]).wait()

    def send_h():
        pltpu.make_async_copy(hs.at[xc], hb.at[xc], hsem.at[0]).start()

        def one(p, k):
            q = (xc + p) % NR

            @pl.when(q // NC != (x + 2) % NX)
            def _():
                copy_x(hs.at[q], hb.at[xc], sh.at[0], hsem.at[0], q).start()
            return k

        lax.fori_loop(1, NR, one, 0)

    lax.fori_loop(0, NT, send_tick, 0)

    load.wait()
    total = NZ * NX * NC * BR
    for q in range(NR):
        for zb in range(NZ):
            r0 = (zb * NX + q // NC) * BR * NC + (BR * NC if q % NC else -2)
            for s in range(2):
                o = zb % 2 * 4 + s * 2
                for j in range(NT):
                    if 0 <= r0 < total:
                        hs[q, zb // 2, j, o:o + 2, :] = fv[s, r0:r0 + 2, 128 * j:128 * j + 128]
                    else:
                        hs[q, zb // 2, j, o:o + 2, :] = jnp.zeros((2, 128), F32)

    send_h()
    lax.fori_loop(NT, HALF, send_tick, 0)

    for cp in tload:
        cp.wait()
    tc = tcol[...].astype(F32)
    to_ = topa[...].astype(F32).reshape(1, -1) * (1.0 / 144.0)
    tabs = []
    for k in range(3):
        tabs.append([jnp.broadcast_to(tc[k:k + 1, 128 * h:128 * h + 128], (8, 128)) for h in range(2)])
    tabs.append([jnp.broadcast_to(to_[:, 128 * h:128 * h + 128], (8, 128)) for h in range(2)])

    def z_copy(zb, up):
        src = fb.at[zb, pl.ds(1, NT), pl.ds(NS if up else 2, 2), pl.ds(TOP, BR), :]
        dst = fb.at[zb, pl.ds(1, NT), pl.ds(0 if up else NS + 2, 2), pl.ds(TOP, BR), :]
        return pltpu.make_async_remote_copy(
            src_ref=src, dst_ref=dst, send_sem=sz.at[int(up)], recv_sem=zsem.at[zb, int(up)],
            device_id=(d + (NR if up else -NR), y), device_id_type=MESH)

    def y_copy(zb, right):
        src = fb.at[zb, NT if right else 1, pl.ds(2, NS), pl.ds(TOP, BR), :]
        dst = fb.at[zb, 0 if right else NT + 1, pl.ds(2, NS), pl.ds(TOP, BR), :]
        return pltpu.make_async_remote_copy(
            src_ref=src, dst_ref=dst, send_sem=sy.at[int(right)], recv_sem=ysem.at[zb, int(right)],
            device_id=(d, y + (1 if right else -1)), device_id_type=MESH)

    def c_copy(zb):
        src = fb.at[zb, pl.ds(1, NT), pl.ds(2, NS), pl.ds(pl.multiple_of(TOP + 8 * (1 - c), 8), 8), :]
        dst = fb.at[zb, pl.ds(1, NT), pl.ds(2, NS), pl.ds(pl.multiple_of((TOP + BR) * c, 8), 8), :]
        return pltpu.make_async_remote_copy(
            src_ref=src, dst_ref=dst, send_sem=sc.at[0], recv_sem=csem.at[zb],
            device_id=(d + 1 - 2 * c, y), device_id_type=MESH)

    def pass_on(zb):
        own = fb.at[zb, pl.ds(1, NT), pl.ds(2, NS), pl.ds(TOP, BR), :]
        pltpu.make_async_copy(own, own, fsem.at[zb]).wait()

        @pl.when(z < NZ - 1)
        def _():
            z_copy(zb, True).start()

        @pl.when(z > 0)
        def _():
            z_copy(zb, False).start()

        @pl.when(y > 0)
        def _():
            y_copy(zb, False).start()

        @pl.when(y < ny - 1)
        def _():
            y_copy(zb, True).start()

        c_copy(zb).start()

    def rows_in(i, k, at):
        @pl.when(i // NC != (x + 2) % NX)
        def _():
            for zb in range(NZ):
                for s in range(2):
                    a = zb % 2 * 4 + s * 2
                    for j in range(NT):
                        fb[zb, j + 1, 2 + 2 * i + s, at:at + 2, :] = hb[i, zb // 2, j, a:a + 2, :]
        return k

    to_x = x + 2 * c - 1

    def o_copy(zb):
        to_b = zb + (to_x + NX) // NX - 1
        return pltpu.make_async_remote_copy(
            src_ref=hp.at[zb], dst_ref=ho.at[to_b], send_sem=so.at[0], recv_sem=osem.at[to_b],
            device_id=((z * NX + (to_x + NX) % NX) * NC + 1 - c, y), device_id_type=MESH)

    def o_goes(zb):
        to_b = zb + (to_x + NX) // NX - 1
        return jnp.logical_and(to_b >= 0, to_b < NZ)

    def o_send(zb):
        for core, at in ((0, TOP), (1, TOP + BR - 2)):
            @pl.when(c == core)
            def _():
                for i in range(4):
                    s = 2 + 2 * NC * ((to_x + 2 + NX) % NX) + i
                    for j in range(NT):
                        hp[zb, j, 2 * i:2 * i + 2, :] = fb[zb, j + 1, s, at:at + 2, :]

        pl.when(o_goes(zb))(lambda: o_copy(zb).start())

    def o_in(zb):
        edge = (1 - c) * (x * NZ + zb) + c * ((NX - 1 - x) * NZ + NZ - 1 - zb) == 0

        @pl.when(edge)
        def _():
            ho[zb] = jnp.zeros((NT, 8, 128), F32)

        @pl.when(jnp.logical_not(edge))
        def _():
            got = ho.at[zb]
            pltpu.make_async_copy(got, got, osem.at[zb]).wait()

        for core, at in ((0, TOP - 2), (1, TOP + BR)):
            @pl.when(c == core)
            def _():
                for i in range(4):
                    s = 2 + 2 * NC * ((x + 2) % NX) + i
                    for j in range(NT):
                        fb[zb, j + 1, s, at:at + 2, :] = ho[zb, j, 2 * i:2 * i + 2, :]

    def all_rows_in():
        near_by = hb.at[pl.ds(0, NR - NC)]
        pltpu.make_async_copy(near_by, near_by, hsem.at[0]).wait()

        @pl.when(c == 0)
        def _():
            lax.fori_loop(0, NR, lambda i, k: rows_in(i, k, TOP - 2), 0)

        @pl.when(c == 1)
        def _():
            lax.fori_loop(0, NR, lambda i, k: rows_in(i, k, TOP + BR), 0)

    def halos(zb):
        @pl.when(z > 0)
        def _():
            z_copy(zb, True).wait_recv()

        @pl.when(z < NZ - 1)
        def _():
            z_copy(zb, False).wait_recv()

        @pl.when(y > 0)
        def _():
            y_copy(zb, True).wait_recv()

        @pl.when(y < ny - 1)
        def _():
            y_copy(zb, False).wait_recv()

        c_copy(zb).wait_recv()

    lane = lax.broadcasted_iota(jnp.int32, (8, 128), 1)
    kd, kr, kc = 0.7 * 0.48 / 12.0, 0.7 * 0.6 / 12.0, 0.7 * 0.64 / 12.0

    def gradients(zb, j, g):
        r = pl.multiple_of(TOP + 8 * g, 8)
        rows = pl.ds(pl.multiple_of(8 * g, 8), 8)
        lanes = pl.ds(pl.multiple_of(128 * j, 128), 128)
        win = [fb[zb, j + 1, s, pl.ds(r, 8), :] for s in range(4)]
        for s in range(NS):
            win.append(fb[zb, j + 1, s + 4, pl.ds(r, 8), :])
            v = win[s + 2]
            gd = 8.0 * (win[s + 3] - win[s + 1]) + (win[s] - win[s + 4])
            m2, m1, p1, p2 = [fb[zb, j + 1, s + 2, pl.ds(r + o, 8), :] for o in (-2, -1, 1, 2)]
            gr = 8.0 * (p1 - m1) + (m2 - p2)
            lt = fb[zb, j, s + 2, pl.ds(r, 8), :]
            rt = fb[zb, j + 2, s + 2, pl.ds(r, 8), :]
            l1 = pltpu.roll(jnp.where(lane == 127, lt, v), 1, 1)
            l2 = pltpu.roll(jnp.where(lane >= 126, lt, v), 2, 1)
            r1 = pltpu.roll(jnp.where(lane == 0, rt, v), 127, 1)
            r2 = pltpu.roll(jnp.where(lane < 2, rt, v), 126, 1)
            gc = 8.0 * (r1 - l1) + (l2 - r2)
            q = gd * gd + gr * gr + gc * gc
            inv = lax.rsqrt(q * (1.0 / 144.0) + 1.0)
            a = q * (inv * inv)
            ga[zb, s, rows, lanes] = a
            gl[zb, s, rows, lanes] = a * (0.3 + jnp.abs(kd * gd + kr * gr + kc * gc) * inv)

    def shade(zb, j, g, m):
        rows = pl.ds(pl.multiple_of(8 * g, 8), 8)
        lanes = pl.ds(pl.multiple_of(128 * j, 128), 128)
        fr = [jnp.zeros((8, 128), F32) for _ in range(3)]
        bk = [jnp.zeros((8, 128), F32) for _ in range(3)]
        tr = jnp.ones((8, 128), F32)
        for s in range(NS):
            ids = bb[zb, s, rows, lanes]
            low = ids & 127
            upper = ids >= 128
            look = [
                jnp.where(upper,
                          jnp.take_along_axis(hi, low, axis=1, mode="promise_in_bounds"),
                          jnp.take_along_axis(lo, low, axis=1, mode="promise_in_bounds"))
                for lo, hi in tabs
            ]
            keep = 1.0 - look[3] * ga[zb, s, rows, lanes]
            w = look[3] * gl[zb, s, rows, lanes]
            for k in range(3):
                col = look[k] * w
                fr[k] = fr[k] + tr * col
                bk[k] = bk[k] * keep + col
            tr = tr * keep
        for k, part in enumerate(fr + bk + [tr]):
            stage[m, k, rows, :] = part

    def i_copy(m):
        zb, j = bin_tile(m)
        return pltpu.make_async_remote_copy(
            src_ref=stage.at[m], dst_ref=img.at[z, j], send_sem=si.at[0], recv_sem=isem.at[j],
            device_id=(zb * NR + xc, y), device_id_type=MESH)

    def finish(m):
        j = m % NT
        img[z, j] = stage[m]
        others = stage.at[pl.ds(0, NZ - 1)]
        pltpu.make_async_copy(others, others, isem.at[j]).wait()
        lanes = pl.ds(pl.multiple_of(128 * j, 128), 128)
        ts = [img[s, j, 6] for s in range(NZ)]
        t = (ts[0] * ts[1]) * (ts[2] * ts[3])
        for n in range(3):
            acc = img[NZ - 1, j, n]
            for s in range(NZ - 2, 0, -1):
                acc = img[s, j, n] + ts[s] * acc
            front[0, n, :, lanes] = img[0, j, n]
            front[1, n, :, lanes] = ts[0] * acc
            acc = img[0, j, 3 + n]
            for s in range(1, NZ - 1):
                acc = img[s, j, 3 + n] + ts[s] * acc
            back[0, n, :, lanes] = img[NZ - 1, j, 3 + n]
            back[1, n, :, lanes] = ts[NZ - 1] * acc
        for part, value in ((0, jnp.zeros_like(t)), (1, t)):
            front[part, 3, :, lanes] = value
            back[part, 3, :, lanes] = value

    def cells_in(n, k):
        pass_on(n)
        o_send(n)
        pl.when(n == 1)(all_rows_in)

        @pl.when(n == NZ - 2)
        def _():
            lax.fori_loop(HALF, HALF + NT, send_tick, 0)

        @pl.when(n == NZ - 1)
        def _():
            lax.fori_loop(HALF + NT, 2 * HALF, send_tick, 0)

        return k

    def shape(n, k):
        halos(n)
        o_in(n)

        def part(h, k2):
            gradients(n, h // 2, h % 2)
            return k2

        lax.fori_loop(0, 2 * NT, part, 0)
        return k

    @pl.when(c == 1)
    def _():
        pl.semaphore_wait(bar, (NZ - 1 + 2) * NC)
        tell(near, 0)

    @pl.when(c == 0)
    def _():
        pl.semaphore_wait(near, 1)

    lax.fori_loop(0, NZ, cells_in, 0)
    lax.fori_loop(0, NZ, shape, 0)

    def wait_all(some, sem):
        pltpu.make_async_copy(some, some, sem).wait()

    def drain():
        ticks_left(0)
        wait_all(hb.at[pl.ds(0, NR - NC - 1)], sh.at[0])
        planes = fb.at[:, pl.ds(1, NT), pl.ds(0, 2), pl.ds(TOP, BR), :]
        sides = fb.at[:, 0, pl.ds(2, NS), pl.ds(TOP, BR), :]
        pl.when(z < NZ - 1)(lambda: wait_all(planes, sz.at[1]))
        pl.when(z > 0)(lambda: wait_all(planes, sz.at[0]))
        pl.when(y > 0)(lambda: wait_all(sides, sy.at[0]))
        pl.when(y < ny - 1)(lambda: wait_all(sides, sy.at[1]))
        wait_all(fb.at[:, pl.ds(1, NT), pl.ds(2, NS), pl.ds(0, 8), :], sc.at[0])
        around = to_x + NX != (to_x + NX) % NX + NX
        pl.when(around)(lambda: wait_all(ho.at[pl.ds(0, NZ - 1)], so.at[0]))
        pl.when(jnp.logical_not(around))(lambda: wait_all(ho, so.at[0]))

    def bins_in(m, k):
        pl.when(m == HALF - NT)(drain)
        zb, j = bin_tile(m)
        got = bb.at[zb, :, :, pl.ds(pl.multiple_of(128 * j, 128), 128)]
        pltpu.make_async_copy(got, got, bsem.at[m]).wait()

        def part(h, k2):
            shade(zb, j, h, m)
            return k2

        lax.fori_loop(0, 2, part, 0)
        pl.when(m < HALF - NT)(lambda: i_copy(m).start())
        pl.when(m >= HALF - NT)(lambda: finish(m))
        return k

    lax.fori_loop(0, HALF, bins_in, 0)

    ticks_left(1)
    wait_all(stage.at[pl.ds(0, HALF - NT)], si.at[0])


def local(field, bin_ids, table_color, table_opacity):
    cols = field.shape[2]
    out = jax.ShapeDtypeStruct((2, 4, BR, cols), F32)
    vm = pl.BlockSpec(memory_space=pltpu.VMEM)
    hbm = pl.BlockSpec(memory_space=pltpu.HBM)
    dma = pltpu.SemaphoreType.DMA
    args = [
        pltpu.with_memory_space_constraint(a, pltpu.HBM)
        for a in (field, bin_ids, table_color, table_opacity)
    ]
    front, back = pl.pallas_call(
        kernel,
        out_shape=(out, out),
        in_specs=[hbm] * 4,
        out_specs=(vm, vm),
        scratch_shapes=[
            pltpu.VMEM(table_color.shape, table_color.dtype),
            pltpu.VMEM(table_opacity.shape, table_opacity.dtype),
            pltpu.VMEM((NZ, NT + 2, NS + 4, BR + 16, 128), F32),
            pltpu.VMEM((NZ, NS, BR, cols), jnp.int32),
            pltpu.VMEM((NR, 2, NT, 8, 128), F32),
            pltpu.VMEM((NR, 2, NT, 8, 128), F32),
            pltpu.VMEM((NZ, NT, 8, 128), F32),
            pltpu.VMEM((NZ, NT, 8, 128), F32),
            pltpu.VMEM(field.shape, F32),
            pltpu.VMEM((NZ, NS, BR, cols), F32),
            pltpu.VMEM((NZ, NS, BR, cols), F32),
            pltpu.VMEM((HALF, 7, BR, 128), F32),
            pltpu.VMEM((NZ, NT, 7, BR, 128), F32),
            dma((3,)), dma((NZ,)), dma((HALF,)), dma((1,)), dma((NZ, 2)), dma((NZ, 2)), dma((NZ,)), dma((NT,)),
            dma((2,)), dma((1,)), dma((2,)), dma((2,)), dma((1,)), dma((1,)), dma((NZ,)), dma((1,)),
            pltpu.SemaphoreType.REGULAR, pltpu.SemaphoreType.REGULAR,
        ],
        compiler_params=pltpu.CompilerParams(
            collective_id=0, has_side_effects=True, vmem_limit_bytes=40 * 2**20),
    )(*args)
    return front[0] + front[1], back[0] + back[1]


def solution(mesh):
    return jax.shard_map(
        local,
        mesh=mesh,
        in_specs=(P("depth", None, "tile"), P("depth", None, "tile"), P(), P()),
        out_specs=(P(None, "depth", "tile"), P(None, "depth", "tile")),
        check_vma=False,
    )
```

```python
import jax
import jax.numpy as jnp
from jax import lax
from jax.experimental import pallas as pl
from jax.experimental.pallas import tpu as pltpu
from jax.sharding import PartitionSpec as P

MESH = pl.DeviceIdType.MESH
F32 = jnp.float32
NZ, NX, NC = 4, 4, 2
NR = NX * NC
NS = 2 * NR
BR = 16
NT = 4
TOP = 8
HALF = NZ * NT


def kernel(
    field, bins, tcol_h, topa_h, front, back,
    tcol, topa, fb, bb, hb, hs, hp, ho, fv, ga, gl, stage, img,
    lsem, fsem, bsem, hsem, zsem, ysem, csem, isem, sx, sh, sz, sy, sc, si, osem, so, ring, near,
):
    d = lax.axis_index("depth")
    y = lax.axis_index("tile")
    ny = lax.axis_size("tile")
    z = d // NR
    xc = d % NR
    x = xc // NC
    c = xc % NC

    load = pltpu.make_async_copy(field, fv, lsem.at[0])
    load.start()
    tload = [pltpu.make_async_copy(tcol_h, tcol, lsem.at[1]), pltpu.make_async_copy(topa_h, topa, lsem.at[2])]
    for cp in tload:
        cp.start()
    bar = pltpu.get_barrier_semaphore()

    def here(z_, x_, c_, y_):
        pl.semaphore_signal(bar, inc=1, device_id=((z_ * NX + x_) * NC + c_, y_), device_id_type=MESH)

    for p in range(1, NX):
        here(z, (x + p) % NX, 0, y)
    pl.when(c == 1)(lambda: here(z, x, 0, y))
    for p in range(1, NZ):
        here((z + p) % NZ, x, 1, y)
    for p in (1, ny - 1):
        here(z, x, 1, (y + p) % ny)

    @pl.when(y == 0)
    def _():
        fb[:, 0, 2:2 + NS, TOP:TOP + BR, :] = jnp.zeros((NZ, NS, BR, 128), F32)

    @pl.when(y == ny - 1)
    def _():
        fb[:, NT + 1, 2:2 + NS, TOP:TOP + BR, :] = jnp.zeros((NZ, NS, BR, 128), F32)

    @pl.when(z == 0)
    def _():
        fb[:, 1:NT + 1, 0:2, TOP:TOP + BR, :] = jnp.zeros((NZ, NT, 2, BR, 128), F32)

    @pl.when(z == NZ - 1)
    def _():
        fb[:, 1:NT + 1, NS + 2:NS + 4, TOP:TOP + BR, :] = jnp.zeros((NZ, NT, 2, BR, 128), F32)

    def tell(sem, c_):
        pl.semaphore_signal(sem, inc=1, device_id=((z * NX + x) * NC + c_, y), device_id_type=MESH)

    @pl.when(c == 0)
    def _():
        pl.semaphore_wait(bar, NR - 1)
        tell(ring, 1)

    @pl.when(c == 1)
    def _():
        pl.semaphore_wait(ring, 1)

    def rows_of(zb, q):
        return pl.ds(pl.multiple_of((zb * NX + q // NC) * BR * NC + q % NC * BR, BR), BR)

    def copy_x(src, dst, send, recv, q):
        return pltpu.make_async_remote_copy(
            src_ref=src, dst_ref=dst, send_sem=send, recv_sem=recv,
            device_id=(z * NR + q, y), device_id_type=MESH)

    def bin_tile(m):
        t = m // NT
        mixed = (t % 3 + 1) // 2
        off = mixed * (1 + 2 * (m % 2)) + (1 - mixed) * 2 * (1 - t // 3)
        return (z + off) % NZ, mixed * ((m - NT) // 2) + (1 - mixed) * (m % NT)

    def tick_refs(n, q):
        f_zb, f_j = n // NT, n % NT
        b_zb, b_j = bin_tile(n - HALF)
        f_cols = pl.ds(pl.multiple_of(128 * f_j, 128), 128)
        b_cols = pl.ds(pl.multiple_of(128 * b_j, 128), 128)
        return (
            (field.at[:, rows_of(f_zb, q), f_cols], fb.at[f_zb, f_j + 1, pl.ds(2 + 2 * xc, 2), pl.ds(TOP, BR), :]),
            (bins.at[:, rows_of(b_zb, q), b_cols], bb.at[b_zb, pl.ds(2 * xc, 2), :, b_cols]),
        )

    def send_tick(n, k=0):
        for kind in range(2):
            @pl.when(n // HALF == kind)
            def _():
                recv = bsem.at[n - HALF] if kind else fsem.at[n // NT]
                src, dst = tick_refs(n, xc)[kind]
                pltpu.make_async_copy(src, dst, recv).start()

                def one(p, k2):
                    q = (xc + p) % NR
                    src, dst = tick_refs(n, q)[kind]
                    copy_x(src, dst, sx.at[kind], recv, q).start()
                    return k2

                lax.fori_loop(1, NR, one, 0)
        return k

    def ticks_left(kind):
        some = bb.at[:, pl.ds(0, NS - 2)]
        pltpu.make_async_copy(some, some, sx.at[kind]).wait()

    def send_h():
        pltpu.make_async_copy(hs.at[xc], hb.at[xc], hsem.at[0]).start()

        def one(p, k):
            q = (xc + p) % NR

            @pl.when(q // NC != (x + 2) % NX)
            def _():
                copy_x(hs.at[q], hb.at[xc], sh.at[0], hsem.at[0], q).start()
            return k

        lax.fori_loop(1, NR, one, 0)

    lax.fori_loop(0, NT, send_tick, 0)

    load.wait()
    total = NZ * NX * NC * BR
    for q in range(NR):
        for zb in range(NZ):
            r0 = (zb * NX + q // NC) * BR * NC + (BR * NC if q % NC else -2)
            for s in range(2):
                o = zb % 2 * 4 + s * 2
                for j in range(NT):
                    if 0 <= r0 < total:
                        hs[q, zb // 2, j, o:o + 2, :] = fv[s, r0:r0 + 2, 128 * j:128 * j + 128]
                    else:
                        hs[q, zb // 2, j, o:o + 2, :] = jnp.zeros((2, 128), F32)

    send_h()
    lax.fori_loop(NT, HALF, send_tick, 0)

    for cp in tload:
        cp.wait()
    tc = (tcol[...].astype(F32) * 8192.0).astype(jnp.int32)
    to_ = (topa[...].astype(F32).reshape(1, -1) * 16384.0).astype(jnp.int32)
    words = [tc[0:1] + tc[1:2] * 16384, tc[2:3] + to_ * 16384]
    tabs = [[jnp.broadcast_to(w[:, 128 * h:128 * h + 128], (8, 128)) for h in range(2)] for w in words]

    def z_copy(zb, up):
        src = fb.at[zb, pl.ds(1, NT), pl.ds(NS if up else 2, 2), pl.ds(TOP, BR), :]
        dst = fb.at[zb, pl.ds(1, NT), pl.ds(0 if up else NS + 2, 2), pl.ds(TOP, BR), :]
        return pltpu.make_async_remote_copy(
            src_ref=src, dst_ref=dst, send_sem=sz.at[int(up)], recv_sem=zsem.at[zb, int(up)],
            device_id=(d + (NR if up else -NR), y), device_id_type=MESH)

    def y_copy(zb, right):
        src = fb.at[zb, NT if right else 1, pl.ds(2, NS), pl.ds(TOP, BR), :]
        dst = fb.at[zb, 0 if right else NT + 1, pl.ds(2, NS), pl.ds(TOP, BR), :]
        return pltpu.make_async_remote_copy(
            src_ref=src, dst_ref=dst, send_sem=sy.at[int(right)], recv_sem=ysem.at[zb, int(right)],
            device_id=(d, y + (1 if right else -1)), device_id_type=MESH)

    def c_copy(zb):
        src = fb.at[zb, pl.ds(1, NT), pl.ds(2, NS), pl.ds(pl.multiple_of(TOP + 8 * (1 - c), 8), 8), :]
        dst = fb.at[zb, pl.ds(1, NT), pl.ds(2, NS), pl.ds(pl.multiple_of((TOP + BR) * c, 8), 8), :]
        return pltpu.make_async_remote_copy(
            src_ref=src, dst_ref=dst, send_sem=sc.at[0], recv_sem=csem.at[zb],
            device_id=(d + 1 - 2 * c, y), device_id_type=MESH)

    def pass_on(zb):
        own = fb.at[zb, pl.ds(1, NT), pl.ds(2, NS), pl.ds(TOP, BR), :]
        pltpu.make_async_copy(own, own, fsem.at[zb]).wait()

        @pl.when(z < NZ - 1)
        def _():
            z_copy(zb, True).start()

        @pl.when(z > 0)
        def _():
            z_copy(zb, False).start()

        @pl.when(y > 0)
        def _():
            y_copy(zb, False).start()

        @pl.when(y < ny - 1)
        def _():
            y_copy(zb, True).start()

        c_copy(zb).start()

    def rows_in(i, k, at):
        @pl.when(i // NC != (x + 2) % NX)
        def _():
            for zb in range(NZ):
                for s in range(2):
                    a = zb % 2 * 4 + s * 2
                    for j in range(NT):
                        fb[zb, j + 1, 2 + 2 * i + s, at:at + 2, :] = hb[i, zb // 2, j, a:a + 2, :]
        return k

    to_x = x + 2 * c - 1

    def o_copy(zb):
        to_b = zb + (to_x + NX) // NX - 1
        return pltpu.make_async_remote_copy(
            src_ref=hp.at[zb], dst_ref=ho.at[to_b], send_sem=so.at[0], recv_sem=osem.at[to_b],
            device_id=((z * NX + (to_x + NX) % NX) * NC + 1 - c, y), device_id_type=MESH)

    def o_goes(zb):
        to_b = zb + (to_x + NX) // NX - 1
        return jnp.logical_and(to_b >= 0, to_b < NZ)

    def o_send(zb):
        for core, at in ((0, TOP), (1, TOP + BR - 2)):
            @pl.when(c == core)
            def _():
                for i in range(4):
                    s = 2 + 2 * NC * ((to_x + 2 + NX) % NX) + i
                    for j in range(NT):
                        hp[zb, j, 2 * i:2 * i + 2, :] = fb[zb, j + 1, s, at:at + 2, :]

        pl.when(o_goes(zb))(lambda: o_copy(zb).start())

    def o_in(zb):
        edge = (1 - c) * (x * NZ + zb) + c * ((NX - 1 - x) * NZ + NZ - 1 - zb) == 0

        @pl.when(edge)
        def _():
            ho[zb] = jnp.zeros((NT, 8, 128), F32)

        @pl.when(jnp.logical_not(edge))
        def _():
            got = ho.at[zb]
            pltpu.make_async_copy(got, got, osem.at[zb]).wait()

        for core, at in ((0, TOP - 2), (1, TOP + BR)):
            @pl.when(c == core)
            def _():
                for i in range(4):
                    s = 2 + 2 * NC * ((x + 2) % NX) + i
                    for j in range(NT):
                        fb[zb, j + 1, s, at:at + 2, :] = ho[zb, j, 2 * i:2 * i + 2, :]

    def all_rows_in():
        near_by = hb.at[pl.ds(0, NR - NC)]
        pltpu.make_async_copy(near_by, near_by, hsem.at[0]).wait()

        @pl.when(c == 0)
        def _():
            lax.fori_loop(0, NR, lambda i, k: rows_in(i, k, TOP - 2), 0)

        @pl.when(c == 1)
        def _():
            lax.fori_loop(0, NR, lambda i, k: rows_in(i, k, TOP + BR), 0)

    def halos(zb):
        @pl.when(z > 0)
        def _():
            z_copy(zb, True).wait_recv()

        @pl.when(z < NZ - 1)
        def _():
            z_copy(zb, False).wait_recv()

        @pl.when(y > 0)
        def _():
            y_copy(zb, True).wait_recv()

        @pl.when(y < ny - 1)
        def _():
            y_copy(zb, False).wait_recv()

        c_copy(zb).wait_recv()

    lane = lax.broadcasted_iota(jnp.int32, (8, 128), 1)
    kd, kr, kc = [0.7 * w / 12.0 / 8192.0 for w in (0.48, 0.6, 0.64)]

    def gradients(zb, j, g):
        r = pl.multiple_of(TOP + 8 * g, 8)
        rows = pl.ds(pl.multiple_of(8 * g, 8), 8)
        lanes = pl.ds(pl.multiple_of(128 * j, 128), 128)
        win = [fb[zb, j + 1, s, pl.ds(r, 8), :] for s in range(4)]
        for s in range(NS):
            win.append(fb[zb, j + 1, s + 4, pl.ds(r, 8), :])
            v = win[s + 2]
            gd = 8.0 * (win[s + 3] - win[s + 1]) + (win[s] - win[s + 4])
            m2, m1, p1, p2 = [fb[zb, j + 1, s + 2, pl.ds(r + o, 8), :] for o in (-2, -1, 1, 2)]
            gr = 8.0 * (p1 - m1) + (m2 - p2)
            lt = fb[zb, j, s + 2, pl.ds(r, 8), :]
            rt = fb[zb, j + 2, s + 2, pl.ds(r, 8), :]
            l1 = pltpu.roll(jnp.where(lane == 127, lt, v), 1, 1)
            l2 = pltpu.roll(jnp.where(lane >= 126, lt, v), 2, 1)
            r1 = pltpu.roll(jnp.where(lane == 0, rt, v), 127, 1)
            r2 = pltpu.roll(jnp.where(lane < 2, rt, v), 126, 1)
            gc = 8.0 * (r1 - l1) + (l2 - r2)
            q = gd * gd + gr * gr + gc * gc
            inv = lax.rsqrt(q * (1.0 / 144.0) + 1.0)
            a = q * (inv * inv) * (1.0 / (144.0 * 16384.0))
            ga[zb, s, rows, lanes] = a
            gl[zb, s, rows, lanes] = a * (0.3 / 8192.0 + jnp.abs(kd * gd + kr * gr + kc * gc) * inv)

    def shade(zb, j, g, m):
        rows = pl.ds(pl.multiple_of(8 * g, 8), 8)
        lanes = pl.ds(pl.multiple_of(128 * j, 128), 128)
        fr = [jnp.zeros((8, 128), F32) for _ in range(3)]
        bk = [jnp.zeros((8, 128), F32) for _ in range(3)]
        tr = jnp.ones((8, 128), F32)
        for s in range(NS):
            ids = bb[zb, s, rows, lanes]
            low = ids & 127
            upper = ids >= 128
            picked = [
                jnp.where(upper,
                          jnp.take_along_axis(hi, low, axis=1, mode="promise_in_bounds"),
                          jnp.take_along_axis(lo, low, axis=1, mode="promise_in_bounds"))
                for lo, hi in tabs
            ]
            look = [f(w).astype(F32) for w in picked for f in (lambda w: w & 16383, lambda w: w >> 14)]
            keep = 1.0 - look[3] * ga[zb, s, rows, lanes]
            w = look[3] * gl[zb, s, rows, lanes]
            for k in range(3):
                col = look[k] * w
                fr[k] = fr[k] + tr * col
                bk[k] = bk[k] * keep + col
            tr = tr * keep
        for k, part in enumerate(fr + bk + [tr]):
            stage[m, k, rows, :] = part

    def i_copy(m):
        zb, j = bin_tile(m)
        return pltpu.make_async_remote_copy(
            src_ref=stage.at[m], dst_ref=img.at[z, j], send_sem=si.at[0], recv_sem=isem.at[j],
            device_id=(zb * NR + xc, y), device_id_type=MESH)

    def finish(m):
        j = m % NT
        img[z, j] = stage[m]
        others = stage.at[pl.ds(0, NZ - 1)]
        pltpu.make_async_copy(others, others, isem.at[j]).wait()
        lanes = pl.ds(pl.multiple_of(128 * j, 128), 128)
        ts = [img[s, j, 6] for s in range(NZ)]
        t = (ts[0] * ts[1]) * (ts[2] * ts[3])
        for n in range(3):
            acc = img[NZ - 1, j, n]
            for s in range(NZ - 2, 0, -1):
                acc = img[s, j, n] + ts[s] * acc
            front[0, n, :, lanes] = img[0, j, n]
            front[1, n, :, lanes] = ts[0] * acc
            acc = img[0, j, 3 + n]
            for s in range(1, NZ - 1):
                acc = img[s, j, 3 + n] + ts[s] * acc
            back[0, n, :, lanes] = img[NZ - 1, j, 3 + n]
            back[1, n, :, lanes] = ts[NZ - 1] * acc
        for part, value in ((0, jnp.zeros_like(t)), (1, t)):
            front[part, 3, :, lanes] = value
            back[part, 3, :, lanes] = value

    def cells_in(n, k):
        pass_on(n)
        o_send(n)
        pl.when(n == 1)(all_rows_in)

        @pl.when(n == NZ - 2)
        def _():
            lax.fori_loop(HALF, HALF + NT, send_tick, 0)

        @pl.when(n == NZ - 1)
        def _():
            lax.fori_loop(HALF + NT, 2 * HALF, send_tick, 0)

        return k

    def shape(n, k):
        halos(n)
        o_in(n)

        def part(h, k2):
            gradients(n, h // 2, h % 2)
            return k2

        lax.fori_loop(0, 2 * NT, part, 0)
        return k

    @pl.when(c == 1)
    def _():
        pl.semaphore_wait(bar, (NZ - 1 + 2) * NC)
        tell(near, 0)

    @pl.when(c == 0)
    def _():
        pl.semaphore_wait(near, 1)

    lax.fori_loop(0, NZ, cells_in, 0)
    lax.fori_loop(0, NZ, shape, 0)

    def wait_all(some, sem):
        pltpu.make_async_copy(some, some, sem).wait()

    def drain():
        ticks_left(0)
        wait_all(hb.at[pl.ds(0, NR - NC - 1)], sh.at[0])
        planes = fb.at[:, pl.ds(1, NT), pl.ds(0, 2), pl.ds(TOP, BR), :]
        sides = fb.at[:, 0, pl.ds(2, NS), pl.ds(TOP, BR), :]
        pl.when(z < NZ - 1)(lambda: wait_all(planes, sz.at[1]))
        pl.when(z > 0)(lambda: wait_all(planes, sz.at[0]))
        pl.when(y > 0)(lambda: wait_all(sides, sy.at[0]))
        pl.when(y < ny - 1)(lambda: wait_all(sides, sy.at[1]))
        wait_all(fb.at[:, pl.ds(1, NT), pl.ds(2, NS), pl.ds(0, 8), :], sc.at[0])
        around = to_x + NX != (to_x + NX) % NX + NX
        pl.when(around)(lambda: wait_all(ho.at[pl.ds(0, NZ - 1)], so.at[0]))
        pl.when(jnp.logical_not(around))(lambda: wait_all(ho, so.at[0]))

    def bins_in(m, k):
        pl.when(m == HALF - NT)(drain)
        zb, j = bin_tile(m)
        got = bb.at[zb, :, :, pl.ds(pl.multiple_of(128 * j, 128), 128)]
        pltpu.make_async_copy(got, got, bsem.at[m]).wait()

        def part(h, k2):
            shade(zb, j, h, m)
            return k2

        lax.fori_loop(0, 2, part, 0)
        pl.when(m < HALF - NT)(lambda: i_copy(m).start())
        pl.when(m >= HALF - NT)(lambda: finish(m))
        return k

    lax.fori_loop(0, HALF, bins_in, 0)

    ticks_left(1)
    wait_all(stage.at[pl.ds(0, HALF - NT)], si.at[0])


def local(field, bin_ids, table_color, table_opacity):
    cols = field.shape[2]
    out = jax.ShapeDtypeStruct((2, 4, BR, cols), F32)
    vm = pl.BlockSpec(memory_space=pltpu.VMEM)
    hbm = pl.BlockSpec(memory_space=pltpu.HBM)
    dma = pltpu.SemaphoreType.DMA
    args = [
        pltpu.with_memory_space_constraint(a, pltpu.HBM)
        for a in (field, bin_ids, table_color, table_opacity)
    ]
    front, back = pl.pallas_call(
        kernel,
        out_shape=(out, out),
        in_specs=[hbm] * 4,
        out_specs=(vm, vm),
        scratch_shapes=[
            pltpu.VMEM(table_color.shape, table_color.dtype),
            pltpu.VMEM(table_opacity.shape, table_opacity.dtype),
            pltpu.VMEM((NZ, NT + 2, NS + 4, BR + 16, 128), F32),
            pltpu.VMEM((NZ, NS, BR, cols), jnp.int32),
            pltpu.VMEM((NR, 2, NT, 8, 128), F32),
            pltpu.VMEM((NR, 2, NT, 8, 128), F32),
            pltpu.VMEM((NZ, NT, 8, 128), F32),
            pltpu.VMEM((NZ, NT, 8, 128), F32),
            pltpu.VMEM(field.shape, F32),
            pltpu.VMEM((NZ, NS, BR, cols), F32),
            pltpu.VMEM((NZ, NS, BR, cols), F32),
            pltpu.VMEM((HALF, 7, BR, 128), F32),
            pltpu.VMEM((NZ, NT, 7, BR, 128), F32),
            dma((3,)), dma((NZ,)), dma((HALF,)), dma((1,)), dma((NZ, 2)), dma((NZ, 2)), dma((NZ,)), dma((NT,)),
            dma((2,)), dma((1,)), dma((2,)), dma((2,)), dma((1,)), dma((1,)), dma((NZ,)), dma((1,)),
            pltpu.SemaphoreType.REGULAR, pltpu.SemaphoreType.REGULAR,
        ],
        compiler_params=pltpu.CompilerParams(
            collective_id=0, has_side_effects=True, vmem_limit_bytes=40 * 2**20),
    )(*args)
    return front[0] + front[1], back[0] + back[1]


def solution(mesh):
    return jax.shard_map(
        local,
        mesh=mesh,
        in_specs=(P("depth", None, "tile"), P("depth", None, "tile"), P(), P()),
        out_specs=(P(None, "depth", "tile"), P(None, "depth", "tile")),
        check_vma=False,
    )
```

```python
import jax
import jax.numpy as jnp
from jax import lax
from jax.experimental import pallas as pl
from jax.experimental.pallas import tpu as pltpu
from jax.sharding import PartitionSpec as P

MESH = pl.DeviceIdType.MESH
F32 = jnp.float32
NZ, NX, NC = 4, 4, 2
NR = NX * NC
NS = 2 * NR
BR = 16
NT = 4
TOP = 8
HALF = NZ * NT


def kernel(
    field, bins, tcol_h, topa_h, front, back,
    tcol, topa, fb, bb, hb, hs, hp, ho, fv, ga, gl, stage, img,
    lsem, fsem, bsem, hsem, zsem, ysem, csem, isem, sx, sh, sz, sy, sc, si, osem, so, ring, near,
):
    d = lax.axis_index("depth")
    y = lax.axis_index("tile")
    ny = lax.axis_size("tile")
    z = d // NR
    xc = d % NR
    x = xc // NC
    c = xc % NC

    bar = pltpu.get_barrier_semaphore()

    def here(z_, x_, c_, y_):
        pl.semaphore_signal(bar, inc=1, device_id=((z_ * NX + x_) * NC + c_, y_), device_id_type=MESH)

    for p in range(1, NX):
        here(z, (x + p) % NX, 0, y)
    pl.when(c == 1)(lambda: here(z, x, 0, y))
    for p in range(1, NZ):
        here((z + p) % NZ, x, 1, y)
    for p in (1, ny - 1):
        here(z, x, 1, (y + p) % ny)

    load = pltpu.make_async_copy(field, fv, lsem.at[0])
    load.start()
    tload = [pltpu.make_async_copy(tcol_h, tcol, lsem.at[1]), pltpu.make_async_copy(topa_h, topa, lsem.at[2])]
    for cp in tload:
        cp.start()

    @pl.when(y == 0)
    def _():
        fb[:, 0, 2:2 + NS, TOP:TOP + BR, :] = jnp.zeros((NZ, NS, BR, 128), F32)

    @pl.when(y == ny - 1)
    def _():
        fb[:, NT + 1, 2:2 + NS, TOP:TOP + BR, :] = jnp.zeros((NZ, NS, BR, 128), F32)

    @pl.when(z == 0)
    def _():
        fb[:, 1:NT + 1, 0:2, TOP:TOP + BR, :] = jnp.zeros((NZ, NT, 2, BR, 128), F32)

    @pl.when(z == NZ - 1)
    def _():
        fb[:, 1:NT + 1, NS + 2:NS + 4, TOP:TOP + BR, :] = jnp.zeros((NZ, NT, 2, BR, 128), F32)

    def tell(sem, c_):
        pl.semaphore_signal(sem, inc=1, device_id=((z * NX + x) * NC + c_, y), device_id_type=MESH)

    @pl.when(c == 0)
    def _():
        pl.semaphore_wait(bar, NR - 1)
        tell(ring, 1)

    @pl.when(c == 1)
    def _():
        pl.semaphore_wait(ring, 1)

    def rows_of(zb, q):
        return pl.ds(pl.multiple_of((zb * NX + q // NC) * BR * NC + q % NC * BR, BR), BR)

    def copy_x(src, dst, send, recv, q):
        return pltpu.make_async_remote_copy(
            src_ref=src, dst_ref=dst, send_sem=send, recv_sem=recv,
            device_id=(z * NR + q, y), device_id_type=MESH)

    def bin_tile(m):
        t = m // NT
        mixed = (t % 3 + 1) // 2
        off = mixed * (1 + 2 * (m % 2)) + (1 - mixed) * 2 * (1 - t // 3)
        return (z + off) % NZ, mixed * ((m - NT) // 2) + (1 - mixed) * (m % NT)

    def tick_refs(n, q):
        f_zb, f_j = n // NT, n % NT
        b_zb, b_j = bin_tile(n - HALF)
        f_cols = pl.ds(pl.multiple_of(128 * f_j, 128), 128)
        b_cols = pl.ds(pl.multiple_of(128 * b_j, 128), 128)
        return (
            (field.at[:, rows_of(f_zb, q), f_cols], fb.at[f_zb, f_j + 1, pl.ds(2 + 2 * xc, 2), pl.ds(TOP, BR), :]),
            (bins.at[:, rows_of(b_zb, q), b_cols], bb.at[b_zb, pl.ds(2 * xc, 2), :, b_cols]),
        )

    def send_tick(n, k=0):
        for kind in range(2):
            @pl.when(n // HALF == kind)
            def _():
                recv = bsem.at[n - HALF] if kind else fsem.at[n // NT]
                src, dst = tick_refs(n, xc)[kind]
                pltpu.make_async_copy(src, dst, recv).start()

                def one(p, k2):
                    q = (xc + p) % NR
                    src, dst = tick_refs(n, q)[kind]
                    copy_x(src, dst, sx.at[kind], recv, q).start()
                    return k2

                lax.fori_loop(1, NR, one, 0)
        return k

    def ticks_left(kind):
        some = bb.at[:, pl.ds(0, NS - 2)]
        pltpu.make_async_copy(some, some, sx.at[kind]).wait()

    def send_h():
        pltpu.make_async_copy(hs.at[xc], hb.at[xc], hsem.at[0]).start()

        def one(p, k):
            q = (xc + p) % NR

            @pl.when(q // NC != (x + 2) % NX)
            def _():
                copy_x(hs.at[q], hb.at[xc], sh.at[0], hsem.at[0], q).start()
            return k

        lax.fori_loop(1, NR, one, 0)

    lax.fori_loop(0, NT, send_tick, 0)

    load.wait()
    total = NZ * NX * NC * BR
    for q in range(NR):
        for zb in range(NZ):
            r0 = (zb * NX + q // NC) * BR * NC + (BR * NC if q % NC else -2)
            for s in range(2):
                o = zb % 2 * 4 + s * 2
                for j in range(NT):
                    if 0 <= r0 < total:
                        hs[q, zb // 2, j, o:o + 2, :] = fv[s, r0:r0 + 2, 128 * j:128 * j + 128]
                    else:
                        hs[q, zb // 2, j, o:o + 2, :] = jnp.zeros((2, 128), F32)

    send_h()
    lax.fori_loop(NT, HALF, send_tick, 0)

    for cp in tload:
        cp.wait()
    tc = (tcol[...].astype(F32) * 8192.0).astype(jnp.int32)
    to_ = (topa[...].astype(F32).reshape(1, -1) * 16384.0).astype(jnp.int32)
    words = [tc[0:1] + tc[1:2] * 16384, tc[2:3] + to_ * 16384]
    tabs = [[jnp.broadcast_to(w[:, 128 * h:128 * h + 128], (8, 128)) for h in range(2)] for w in words]

    def z_copy(zb, up):
        src = fb.at[zb, pl.ds(1, NT), pl.ds(NS if up else 2, 2), pl.ds(TOP, BR), :]
        dst = fb.at[zb, pl.ds(1, NT), pl.ds(0 if up else NS + 2, 2), pl.ds(TOP, BR), :]
        return pltpu.make_async_remote_copy(
            src_ref=src, dst_ref=dst, send_sem=sz.at[int(up)], recv_sem=zsem.at[zb, int(up)],
            device_id=(d + (NR if up else -NR), y), device_id_type=MESH)

    def y_copy(zb, right):
        src = fb.at[zb, NT if right else 1, pl.ds(2, NS), pl.ds(TOP, BR), :]
        dst = fb.at[zb, 0 if right else NT + 1, pl.ds(2, NS), pl.ds(TOP, BR), :]
        return pltpu.make_async_remote_copy(
            src_ref=src, dst_ref=dst, send_sem=sy.at[int(right)], recv_sem=ysem.at[zb, int(right)],
            device_id=(d, y + (1 if right else -1)), device_id_type=MESH)

    def c_copy(zb):
        src = fb.at[zb, pl.ds(1, NT), pl.ds(2, NS), pl.ds(pl.multiple_of(TOP + 8 * (1 - c), 8), 8), :]
        dst = fb.at[zb, pl.ds(1, NT), pl.ds(2, NS), pl.ds(pl.multiple_of((TOP + BR) * c, 8), 8), :]
        return pltpu.make_async_remote_copy(
            src_ref=src, dst_ref=dst, send_sem=sc.at[0], recv_sem=csem.at[zb],
            device_id=(d + 1 - 2 * c, y), device_id_type=MESH)

    def pass_on(zb):
        own = fb.at[zb, pl.ds(1, NT), pl.ds(2, NS), pl.ds(TOP, BR), :]
        pltpu.make_async_copy(own, own, fsem.at[zb]).wait()

        @pl.when(z < NZ - 1)
        def _():
            z_copy(zb, True).start()

        @pl.when(z > 0)
        def _():
            z_copy(zb, False).start()

        @pl.when(y > 0)
        def _():
            y_copy(zb, False).start()

        @pl.when(y < ny - 1)
        def _():
            y_copy(zb, True).start()

        c_copy(zb).start()

    def rows_in(i, k, at):
        @pl.when(i // NC != (x + 2) % NX)
        def _():
            for zb in range(NZ):
                for s in range(2):
                    a = zb % 2 * 4 + s * 2
                    for j in range(NT):
                        fb[zb, j + 1, 2 + 2 * i + s, at:at + 2, :] = hb[i, zb // 2, j, a:a + 2, :]
        return k

    to_x = x + 2 * c - 1

    def o_copy(zb):
        to_b = zb + (to_x + NX) // NX - 1
        return pltpu.make_async_remote_copy(
            src_ref=hp.at[zb], dst_ref=ho.at[to_b], send_sem=so.at[0], recv_sem=osem.at[to_b],
            device_id=((z * NX + (to_x + NX) % NX) * NC + 1 - c, y), device_id_type=MESH)

    def o_goes(zb):
        to_b = zb + (to_x + NX) // NX - 1
        return jnp.logical_and(to_b >= 0, to_b < NZ)

    def o_send(zb):
        for core, at in ((0, TOP), (1, TOP + BR - 2)):
            @pl.when(c == core)
            def _():
                for i in range(4):
                    s = 2 + 2 * NC * ((to_x + 2 + NX) % NX) + i
                    for j in range(NT):
                        hp[zb, j, 2 * i:2 * i + 2, :] = fb[zb, j + 1, s, at:at + 2, :]

        pl.when(o_goes(zb))(lambda: o_copy(zb).start())

    def o_in(zb):
        edge = (1 - c) * (x * NZ + zb) + c * ((NX - 1 - x) * NZ + NZ - 1 - zb) == 0

        @pl.when(edge)
        def _():
            ho[zb] = jnp.zeros((NT, 8, 128), F32)

        @pl.when(jnp.logical_not(edge))
        def _():
            got = ho.at[zb]
            pltpu.make_async_copy(got, got, osem.at[zb]).wait()

        for core, at in ((0, TOP - 2), (1, TOP + BR)):
            @pl.when(c == core)
            def _():
                for i in range(4):
                    s = 2 + 2 * NC * ((x + 2) % NX) + i
                    for j in range(NT):
                        fb[zb, j + 1, s, at:at + 2, :] = ho[zb, j, 2 * i:2 * i + 2, :]

    def all_rows_in():
        near_by = hb.at[pl.ds(0, NR - NC)]
        pltpu.make_async_copy(near_by, near_by, hsem.at[0]).wait()

        @pl.when(c == 0)
        def _():
            lax.fori_loop(0, NR, lambda i, k: rows_in(i, k, TOP - 2), 0)

        @pl.when(c == 1)
        def _():
            lax.fori_loop(0, NR, lambda i, k: rows_in(i, k, TOP + BR), 0)

    def halos(zb):
        @pl.when(z > 0)
        def _():
            z_copy(zb, True).wait_recv()

        @pl.when(z < NZ - 1)
        def _():
            z_copy(zb, False).wait_recv()

        @pl.when(y > 0)
        def _():
            y_copy(zb, True).wait_recv()

        @pl.when(y < ny - 1)
        def _():
            y_copy(zb, False).wait_recv()

        c_copy(zb).wait_recv()

    lane = lax.broadcasted_iota(jnp.int32, (8, 128), 1)
    kd, kr, kc = [0.7 * w / 12.0 / 8192.0 for w in (0.48, 0.6, 0.64)]

    def gradients(zb, j, g):
        r = pl.multiple_of(TOP + 8 * g, 8)
        rows = pl.ds(pl.multiple_of(8 * g, 8), 8)
        lanes = pl.ds(pl.multiple_of(128 * j, 128), 128)
        win = [fb[zb, j + 1, s, pl.ds(r, 8), :] for s in range(4)]
        for s in range(NS):
            win.append(fb[zb, j + 1, s + 4, pl.ds(r, 8), :])
            v = win[s + 2]
            gd = 8.0 * (win[s + 3] - win[s + 1]) + (win[s] - win[s + 4])
            m2, m1, p1, p2 = [fb[zb, j + 1, s + 2, pl.ds(r + o, 8), :] for o in (-2, -1, 1, 2)]
            gr = 8.0 * (p1 - m1) + (m2 - p2)
            lt = fb[zb, j, s + 2, pl.ds(r, 8), :]
            rt = fb[zb, j + 2, s + 2, pl.ds(r, 8), :]
            l1 = pltpu.roll(jnp.where(lane == 127, lt, v), 1, 1)
            l2 = pltpu.roll(jnp.where(lane >= 126, lt, v), 2, 1)
            r1 = pltpu.roll(jnp.where(lane == 0, rt, v), 127, 1)
            r2 = pltpu.roll(jnp.where(lane < 2, rt, v), 126, 1)
            gc = 8.0 * (r1 - l1) + (l2 - r2)
            q = gd * gd + gr * gr + gc * gc
            inv = lax.rsqrt(q * (1.0 / 144.0) + 1.0)
            a = q * (inv * inv) * (1.0 / (144.0 * 16384.0))
            ga[zb, s, rows, lanes] = a
            gl[zb, s, rows, lanes] = a * (0.3 / 8192.0 + jnp.abs(kd * gd + kr * gr + kc * gc) * inv)

    def shade(zb, j, g, m):
        rows = pl.ds(pl.multiple_of(8 * g, 8), 8)
        lanes = pl.ds(pl.multiple_of(128 * j, 128), 128)
        fr = [jnp.zeros((8, 128), F32) for _ in range(3)]
        bk = [jnp.zeros((8, 128), F32) for _ in range(3)]
        tr = jnp.ones((8, 128), F32)
        for s in range(NS):
            ids = bb[zb, s, rows, lanes]
            low = ids & 127
            upper = ids >= 128
            picked = [
                jnp.where(upper,
                          jnp.take_along_axis(hi, low, axis=1, mode="promise_in_bounds"),
                          jnp.take_along_axis(lo, low, axis=1, mode="promise_in_bounds"))
                for lo, hi in tabs
            ]
            look = [f(w).astype(F32) for w in picked for f in (lambda w: w & 16383, lambda w: w >> 14)]
            keep = 1.0 - look[3] * ga[zb, s, rows, lanes]
            w = look[3] * gl[zb, s, rows, lanes]
            for k in range(3):
                col = look[k] * w
                fr[k] = fr[k] + tr * col
                bk[k] = bk[k] * keep + col
            tr = tr * keep
        for k, part in enumerate(fr + bk + [tr]):
            stage[m, k, rows, :] = part

    def i_copy(m):
        zb, j = bin_tile(m)
        return pltpu.make_async_remote_copy(
            src_ref=stage.at[m], dst_ref=img.at[z, j], send_sem=si.at[0], recv_sem=isem.at[j],
            device_id=(zb * NR + xc, y), device_id_type=MESH)

    def finish(m):
        j = m % NT
        img[z, j] = stage[m]
        others = stage.at[pl.ds(0, NZ - 1)]
        pltpu.make_async_copy(others, others, isem.at[j]).wait()
        lanes = pl.ds(pl.multiple_of(128 * j, 128), 128)
        ts = [img[s, j, 6] for s in range(NZ)]
        t = (ts[0] * ts[1]) * (ts[2] * ts[3])
        for n in range(3):
            acc = img[NZ - 1, j, n]
            for s in range(NZ - 2, 0, -1):
                acc = img[s, j, n] + ts[s] * acc
            front[0, n, :, lanes] = img[0, j, n]
            front[1, n, :, lanes] = ts[0] * acc
            acc = img[0, j, 3 + n]
            for s in range(1, NZ - 1):
                acc = img[s, j, 3 + n] + ts[s] * acc
            back[0, n, :, lanes] = img[NZ - 1, j, 3 + n]
            back[1, n, :, lanes] = ts[NZ - 1] * acc
        for part, value in ((0, jnp.zeros_like(t)), (1, t)):
            front[part, 3, :, lanes] = value
            back[part, 3, :, lanes] = value

    def cells_in(n, k):
        pass_on(n)
        o_send(n)
        pl.when(n == 1)(all_rows_in)

        @pl.when(n == NZ - 2)
        def _():
            lax.fori_loop(HALF, HALF + NT, send_tick, 0)

        @pl.when(n == NZ - 1)
        def _():
            lax.fori_loop(HALF + NT, 2 * HALF, send_tick, 0)

        return k

    def shape(n, k):
        halos(n)
        o_in(n)

        def part(h, k2):
            gradients(n, h // 2, h % 2)
            return k2

        lax.fori_loop(0, 2 * NT, part, 0)
        return k

    @pl.when(c == 1)
    def _():
        pl.semaphore_wait(bar, (NZ - 1 + 2) * NC)
        tell(near, 0)

    @pl.when(c == 0)
    def _():
        pl.semaphore_wait(near, 1)

    lax.fori_loop(0, NZ, cells_in, 0)
    lax.fori_loop(0, NZ, shape, 0)

    def wait_all(some, sem):
        pltpu.make_async_copy(some, some, sem).wait()

    def drain():
        ticks_left(0)
        wait_all(hb.at[pl.ds(0, NR - NC - 1)], sh.at[0])
        planes = fb.at[:, pl.ds(1, NT), pl.ds(0, 2), pl.ds(TOP, BR), :]
        sides = fb.at[:, 0, pl.ds(2, NS), pl.ds(TOP, BR), :]
        pl.when(z < NZ - 1)(lambda: wait_all(planes, sz.at[1]))
        pl.when(z > 0)(lambda: wait_all(planes, sz.at[0]))
        pl.when(y > 0)(lambda: wait_all(sides, sy.at[0]))
        pl.when(y < ny - 1)(lambda: wait_all(sides, sy.at[1]))
        wait_all(fb.at[:, pl.ds(1, NT), pl.ds(2, NS), pl.ds(0, 8), :], sc.at[0])
        around = to_x + NX != (to_x + NX) % NX + NX
        pl.when(around)(lambda: wait_all(ho.at[pl.ds(0, NZ - 1)], so.at[0]))
        pl.when(jnp.logical_not(around))(lambda: wait_all(ho, so.at[0]))

    def bins_in(m, k):
        pl.when(m == HALF - NT)(drain)
        zb, j = bin_tile(m)
        got = bb.at[zb, :, :, pl.ds(pl.multiple_of(128 * j, 128), 128)]
        pltpu.make_async_copy(got, got, bsem.at[m]).wait()

        def part(h, k2):
            shade(zb, j, h, m)
            return k2

        lax.fori_loop(0, 2, part, 0)
        pl.when(m < HALF - NT)(lambda: i_copy(m).start())
        pl.when(m >= HALF - NT)(lambda: finish(m))
        return k

    lax.fori_loop(0, HALF, bins_in, 0)

    ticks_left(1)
    wait_all(stage.at[pl.ds(0, HALF - NT)], si.at[0])


def local(field, bin_ids, table_color, table_opacity):
    cols = field.shape[2]
    out = jax.ShapeDtypeStruct((2, 4, BR, cols), F32)
    vm = pl.BlockSpec(memory_space=pltpu.VMEM)
    hbm = pl.BlockSpec(memory_space=pltpu.HBM)
    dma = pltpu.SemaphoreType.DMA
    args = [
        pltpu.with_memory_space_constraint(a, pltpu.HBM)
        for a in (field, bin_ids, table_color, table_opacity)
    ]
    front, back = pl.pallas_call(
        kernel,
        out_shape=(out, out),
        in_specs=[hbm] * 4,
        out_specs=(vm, vm),
        scratch_shapes=[
            pltpu.VMEM(table_color.shape, table_color.dtype),
            pltpu.VMEM(table_opacity.shape, table_opacity.dtype),
            pltpu.VMEM((NZ, NT + 2, NS + 4, BR + 16, 128), F32),
            pltpu.VMEM((NZ, NS, BR, cols), jnp.int32),
            pltpu.VMEM((NR, 2, NT, 8, 128), F32),
            pltpu.VMEM((NR, 2, NT, 8, 128), F32),
            pltpu.VMEM((NZ, NT, 8, 128), F32),
            pltpu.VMEM((NZ, NT, 8, 128), F32),
            pltpu.VMEM(field.shape, F32),
            pltpu.VMEM((NZ, NS, BR, cols), F32),
            pltpu.VMEM((NZ, NS, BR, cols), F32),
            pltpu.VMEM((HALF, 7, BR, 128), F32),
            pltpu.VMEM((NZ, NT, 7, BR, 128), F32),
            dma((3,)), dma((NZ,)), dma((HALF,)), dma((1,)), dma((NZ, 2)), dma((NZ, 2)), dma((NZ,)), dma((NT,)),
            dma((2,)), dma((1,)), dma((2,)), dma((2,)), dma((1,)), dma((1,)), dma((NZ,)), dma((1,)),
            pltpu.SemaphoreType.REGULAR, pltpu.SemaphoreType.REGULAR,
        ],
        compiler_params=pltpu.CompilerParams(
            collective_id=0, has_side_effects=True, vmem_limit_bytes=40 * 2**20),
    )(*args)
    return front[0] + front[1], back[0] + back[1]


def solution(mesh):
    return jax.shard_map(
        local,
        mesh=mesh,
        in_specs=(P("depth", None, "tile"), P("depth", None, "tile"), P(), P()),
        out_specs=(P(None, "depth", "tile"), P(None, "depth", "tile")),
        check_vma=False,
    )
```
